128 devices in a mesh: group: 4 (over y_lo, core), blk: 32 (over y_hi, x, z).
Axes of the slice: x: 4, y: 4 (y_hi: 2, y_lo: 2; y = y_hi * 2 + y_lo), z: 4, core: 2. Of those that a mesh axis runs over, the one named last changes fastest.
Arguments:
- embeddings: float32 [49152, 1024], P(('group', 'blk'))
- ranks: int32 [49152], P(('group', 'blk')), may hold values from 0 to 49151, each once
- routes: int32 [49152, 1], P(('group', 'blk')), may hold values from 0 to 127; in each aligned block of 384 rows (0 to 383, 384 to 767, ...) at most 6 rows name the same one
Outputs:
- earlier_max: float32 [49152], P(('group', 'blk'))
- later_max: float32 [49152], P(('group', 'blk'))
The draws below stay inside these ranges and needn't reach their ends.
Inputs may be any that keep to these rules, and one draw needn't show every extreme that they name: `routes`: among the 384 documents of one source shard at most 6 name the same member block; some shard's documents name some block exactly 6 times.
All inputs are finite; a program needn't handle non-finite values.
Results may differ from the reference program's by a relative error of at most 0.0003.
Values may be sent and summed in bfloat16 or wider, within the bound.
A program may use at most 64 MiB of HBM per device.

```python
import math
import jax
import jax.numpy as jnp
import numpy as np
from jax import lax

D = 1024
R_DEV = 384
STEPS = 4
ROWS = 49152
N_GROUP = 4
N_BLK = 32


def draw_embeddings(key, part):
    key = jax.random.fold_in(key, 7)
    key_noise, key_dir, key_str = jax.random.split(key, 3)
    direction = jax.random.normal(key_dir, (1, D), jnp.float32)
    noise_rows = jnp.clip(jax.random.normal(key_noise, (ROWS, D), jnp.float32), -5.0, 5.0)
    strength = jax.random.uniform(key_str, (ROWS, 1), jnp.float32, 0.0, 2.0)
    return noise_rows + strength * direction


def deal_out(key, own, number, rows, number_of, top, bound, slope):
    order = jax.random.permutation(key, number_of)
    crowded, ordinary = shares(number_of, rows * top, bound, slope, True), shares(number_of, rows * top, bound, slope, False)
    places = jnp.arange(number_of)

    def named(sizes, rotation):
        used = int((sizes > 0).sum())
        fixed = max(1, used // 4)
        shifted = fixed + (places - fixed + rotation * (used - fixed)) % max(1, number_of - fixed)
        return jnp.zeros((number_of,), jnp.int32).at[order[jnp.where(places < fixed, places, shifted)]].set(jnp.asarray(sizes, jnp.int32))

    sizes = jnp.where(number % 4 == 0, named(crowded, number // 4), named(ordinary, number - number // 4 - 1))
    mixed = jax.random.permutation(jax.random.fold_in(own, 3), number_of)
    donor, sink = mixed[0:number_of // 2 * 2:2], mixed[1:number_of // 2 * 2:2]
    room = jnp.minimum(sizes[donor] - 1, bound - sizes[sink]) // 2
    room = jnp.where((donor == order[0]) | (sink == order[0]) | (sizes[sink] == 0), 0, jnp.maximum(room, 0))
    shifted = jax.random.randint(jax.random.fold_in(own, 4), (number_of // 2,), 0, 1 << 20) % (room + 1)
    sizes = sizes.at[donor].add(-shifted).at[sink].add(shifted)
    items = jnp.searchsorted(jnp.cumsum(sizes), jnp.arange(rows * top), side="right").astype(jnp.int32)
    listing = items.reshape(top, rows).T
    listing = listing[jax.random.permutation(jax.random.fold_in(own, 1), rows)]
    rotation = jax.random.randint(jax.random.fold_in(own, 2), (rows, 1), 0, top)
    return jnp.take_along_axis(listing, (jnp.arange(top)[None, :] + rotation) % top, axis=1)


def shares(number_of, total, reach, lean, full):
    weights = [(1 << 20) // math.isqrt(standing ** lean) + 1 for standing in range(1, number_of + 1)]
    largest = reach if full else min(reach, max(-(-total // number_of), total * weights[0] // sum(weights)))
    least = 1 if total - largest >= number_of - 1 else 0
    given, spare = [largest] + [least] * (number_of - 1), total - largest - least * (number_of - 1)
    while spare > 0:
        movable = [i for i in range(1, number_of) if given[i] < largest] or [i for i in range(1, number_of) if given[i] < reach]
        mass, budget = sum([weights[i] for i in movable]), spare
        for i in movable:
            addition = min(reach - given[i], max(1, budget * weights[i] // mass), spare)
            given[i] = given[i] + addition
            spare = spare - addition
    return np.array(given)


def setup_inputs(seed: int = 0) -> dict:
    streams_of = jax.random.split(jax.random.key(seed), 4)
    embeddings = draw_embeddings(jax.random.fold_in(streams_of[3], 71), 0)
    ranks = jax.random.permutation(streams_of[1], ROWS).astype(jnp.int32)
    routes_keys = jax.random.split(jax.random.fold_in(streams_of[2], 1), ROWS // R_DEV)
    routes_turns = jax.random.permutation(jax.random.fold_in(streams_of[2], 3), ROWS // R_DEV)
    routes = jax.vmap(lambda own, number: deal_out(jax.random.fold_in(streams_of[2], 2), own, number, R_DEV, N_GROUP * N_BLK, 1, 2 * R_DEV // (N_GROUP * N_BLK), 1))(routes_keys, routes_turns).reshape((ROWS, 1))
    return dict(embeddings=embeddings, ranks=ranks, routes=routes)


def unit_rows(embeddings):
    mean_square = lax.optimization_barrier(jnp.mean(embeddings * embeddings, axis=-1, keepdims=True))
    return (embeddings * lax.rsqrt(mean_square + 1e-06) * D ** (-0.5)).astype(jnp.bfloat16)

def compare(left, left_rank, right, right_rank):
    scores = jnp.dot(left.astype(jnp.float32), right.astype(jnp.float32).T, precision=lax.Precision.HIGHEST)
    valid = (left_rank[:, None] >= 0) & (right_rank[None, :] >= 0)
    lower = valid & (right_rank[None, :] < left_rank[:, None])
    higher = valid & (right_rank[None, :] > left_rank[:, None])
    low_scores = jnp.where(lower, scores, -1.0)
    high_scores = jnp.where(higher, scores, -1.0)
    return (low_scores.max(1), high_scores.max(1), high_scores.max(0), low_scores.max(0))

def reference(embeddings, ranks, routes):
    total_devs = N_GROUP * N_BLK
    slot_count = 2 * R_DEV
    capacity = slot_count // total_devs
    unit = unit_rows(embeddings)
    target = routes[:, 0]
    one_hot = (target.reshape(total_devs, R_DEV)[:, :, None] == jnp.arange(total_devs, dtype=jnp.int32)[None, None, :]).astype(jnp.int32)
    earlier_count = jnp.cumsum(one_hot, axis=1) - one_hot
    slot_index = lax.optimization_barrier(jnp.sum(earlier_count * one_hot, axis=2)).reshape(-1)
    source = jnp.arange(ROWS, dtype=jnp.int32) // R_DEV
    position = target * slot_count + source * capacity + slot_index
    blocks = jnp.zeros((total_devs * slot_count, D), jnp.bfloat16).at[position].set(unit).reshape(total_devs, slot_count, D)
    block_ranks = jnp.full((total_devs * slot_count,), -1, jnp.int32).at[position].set(ranks).reshape(total_devs, slot_count)

    def per_device(device):
        group_index = device // N_BLK
        block_index = device % N_BLK
        left = blocks[device]
        left_rank = block_ranks[device]
        mine_early, mine_late, other_early, other_late = ([], [], [], [])
        for offset in range(STEPS + 1):
            other = group_index * N_BLK + (block_index - offset) % N_BLK
            left_early, left_late, right_early, right_late = compare(left, left_rank, blocks[other], block_ranks[other])
            mine_early.append(left_early)
            mine_late.append(left_late)
            other_early.append(right_early)
            other_late.append(right_late)
        return (jnp.stack(mine_early), jnp.stack(mine_late), jnp.stack(other_early), jnp.stack(other_late))
    mine_early, mine_late, other_early, other_late = lax.map(per_device, jnp.arange(total_devs, dtype=jnp.int32))
    early_total = mine_early.max(1).reshape(N_GROUP, N_BLK, slot_count)
    late_total = mine_late.max(1).reshape(N_GROUP, N_BLK, slot_count)
    other_early = other_early.reshape(N_GROUP, N_BLK, STEPS + 1, slot_count)
    other_late = other_late.reshape(N_GROUP, N_BLK, STEPS + 1, slot_count)
    for offset in range(STEPS + 1):
        early_total = jnp.maximum(early_total, jnp.roll(other_early[:, :, offset], -offset, axis=1))
        late_total = jnp.maximum(late_total, jnp.roll(other_late[:, :, offset], -offset, axis=1))
    earlier_max = early_total.reshape(-1)[position]
    later_max = late_total.reshape(-1)[position]
    return (earlier_max, later_max)
```

```python
import jax
import jax.numpy as jnp
from jax import lax
from jax.experimental import pallas as pl
from jax.experimental.pallas import tpu as pltpu
from jax.sharding import PartitionSpec as P

MESH = pl.DeviceIdType.MESH
F32 = jnp.float32
BF16 = jnp.bfloat16

D = 1024
ROWS = 384
SLOTS = 768
CH = 3
CR = 256
COL = 8
PLANE = 16


def iota(shape, dim):
    return lax.broadcasted_iota(jnp.int32, shape, dim)


def hot(mask):
    return jnp.where(mask, 1.0, 0.0).astype(BF16)


def pick(x, onehot, parts):
    rows = x.shape[0]
    pieces = []
    for _ in range(parts):
        piece = x.astype(BF16)
        pieces.append(piece)
        x = x - piece.astype(F32)
    out = jnp.dot(jnp.concatenate(pieces, axis=0), onehot, preferred_element_type=F32)
    total = out[(parts - 1) * rows :]
    for p in range(parts - 2, -1, -1):
        total = total + out[p * rows : (p + 1) * rows]
    return total


def place(x, z):
    return x * 4 + jnp.where(x % 2 == 0, z, 3 - z)


def chip(s):
    x = s // 4
    z = s % 4
    return x, jnp.where(x % 2 == 0, z, 3 - z)


def device(x, y, z, core):
    return ((y % 2) * 2 + core, (y // 2) * 16 + x * 4 + z)


def kernel(
    emb, meta, out_early, out_late,
    send1, recv1, send2, own, left, right,
    rk1s, rk1r, rk2s, rk2r, rk_own, rk_left, rk_right,
    lr_own, lr_left, acc_left, acc_right,
    part_s, part_r, b1s, b1r, b2s, b2r, m_home, m_back,
    ss1, rs1, ss2, rs2, ssr1, rsr1, ssr2, rsr2, ssring, rsring, ssrk, rsrk,
    sspart, rspart, ssb1, rsb1, ssb2, rsb2, loc1, loc2,
):
    grp = lax.axis_index("group")
    blk = lax.axis_index("blk")
    x, y, z, core = (blk // 4) % 4, (blk // 16) * 2 + grp // 2, blk % 4, grp % 2
    me = y * 2 + core
    s = place(x, z)

    def col_dev(g):
        return device(x, g // 2, z, g % 2)

    def ring_dev(t, k):
        tx, tz = chip(t)
        return device(tx, y, tz, k)

    up = (s + 1) % PLANE
    down = (s + PLANE - 1) % PLANE
    diag = ring_dev(jnp.where(core == 0, down, up), 1 - core)
    sibling = ring_dev(s, 1 - core)

    barrier = pltpu.get_barrier_semaphore()

    def greet_col(i, c):
        pl.semaphore_signal(barrier, inc=1, device_id=col_dev((me + i) % COL), device_id_type=MESH)
        return c

    def greet_plane(i, c):
        pl.semaphore_signal(barrier, inc=1, device_id=ring_dev((s + i) % PLANE, core), device_id_type=MESH)
        return c

    lax.fori_loop(1, COL, greet_col, 0)
    lax.fori_loop(1, PLANE, greet_plane, 0)
    pl.semaphore_signal(barrier, inc=1, device_id=diag, device_id_type=MESH)

    e = emb[...]
    mean_square = jnp.mean(e * e, axis=-1, keepdims=True)
    unit = (e * lax.rsqrt(mean_square + 1e-06) * D ** (-0.5)).astype(BF16)
    target = meta[0:1, :]
    rank = meta[1:2, :].astype(F32) + 1.0
    spread = iota((128, ROWS), 0) == target
    before = hot(iota((ROWS, ROWS), 0) < iota((ROWS, ROWS), 1))
    count = jnp.dot(hot(spread), before, preferred_element_type=F32)
    slot = jnp.sum(jnp.where(spread, count, 0.0), axis=0, keepdims=True).astype(jnp.int32)
    block = target % 32
    goal = (target // 32) * 2 + block % 2
    ring = block // 2
    chunk = slot // 2
    at_goal = iota((COL, ROWS), 0) == goal
    spot = chunk * 32 + ring * 2 + slot % 2
    at_spot = hot(iota((128, ROWS), 0) == spot)
    ranks16 = jnp.concatenate([jnp.where(at_goal, rank, 0.0), jnp.zeros((COL, ROWS), F32)], axis=0)
    hi = ranks16.astype(BF16)
    lo = (ranks16 - hi.astype(F32)).astype(BF16)
    dims = (((1,), (1,)), ((), ()))
    packed = lax.dot_general(hi, at_spot, dims, preferred_element_type=F32) + lax.dot_general(
        lo, at_spot, dims, preferred_element_type=F32
    )
    for g in range(COL):
        rk1s[g] = packed[g : g + 1]

    def fill(q):
        index = jnp.where(chunk == q, goal * 32 + ring * 2 + slot % 2, -1)
        select = hot(iota((CR, ROWS), 0) == index)
        for n in range(4):
            cols = slice(n * 256, (n + 1) * 256)
            rows = jnp.dot(select, unit[:, cols], preferred_element_type=F32).astype(BF16)
            send1[q, :, :, cols] = rows.reshape(COL, 32, 256)

    fill(0)
    pl.semaphore_wait(barrier, COL - 1 + PLANE - 1 + 1)

    def rk1(i):
        g = (me + i) % COL
        return pltpu.make_async_remote_copy(
            src_ref=rk1s.at[g], dst_ref=rk1r.at[me], send_sem=ssr1.at[i], recv_sem=rsr1.at[i],
            device_id=col_dev(g), device_id_type=MESH,
        )

    def row1(q, i):
        g = (me + i) % COL
        return pltpu.make_async_remote_copy(
            src_ref=send1.at[q, g], dst_ref=recv1.at[q, me], send_sem=ss1.at[q, i], recv_sem=rs1.at[q, i],
            device_id=col_dev(g), device_id_type=MESH,
        )

    def row2(q, i):
        t = (s + i) % PLANE
        return pltpu.make_async_remote_copy(
            src_ref=send2.at[q, t], dst_ref=own.at[q, s], send_sem=ss2.at[q, i], recv_sem=rs2.at[q, i],
            device_id=ring_dev(t, core), device_id_type=MESH,
        )

    def rk2(i):
        t = (s + i) % PLANE
        return pltpu.make_async_remote_copy(
            src_ref=rk2s.at[t], dst_ref=rk2r.at[s], send_sem=ssr2.at[i], recv_sem=rsr2.at[i],
            device_id=ring_dev(t, core), device_id_type=MESH,
        )

    def each(first, last, act):
        def step(i, c):
            act(i)
            return c

        lax.fori_loop(first, last, step, 0)

    each(1, COL, lambda i: rk1(i).start())
    for q in range(CH):
        if q:
            fill(q)
        each(1, COL, lambda i: row1(q, i).start())
        pltpu.make_async_copy(send1.at[q, me], recv1.at[q, me], loc1.at[q]).start()

    rk1r[me] = rk1s[me]
    each(1, COL, lambda i: rk1(i).wait_recv())
    seen = jnp.concatenate([rk1r[g] for g in range(COL)], axis=0)
    lane = iota((PLANE, COL, 128), 2)
    wide = jnp.where((lane % 32) // 2 == iota((PLANE, COL, 128), 0), seen[None], 0.0)
    a, b = iota((128, 128), 0), iota((128, 128), 1)
    fold = hot((a // 32 == b // 16) & (a % 2 == b % 2) & (a < 96) & (b < 48))
    wide = pick(wide.reshape(128, 128), fold, 2).reshape(PLANE, COL, 128)
    wide = jnp.sum(jnp.where((lane % 16) // 2 == iota((PLANE, COL, 128), 1), wide, 0.0), axis=1)
    for t in range(PLANE):
        rk2s[t] = wide[t : t + 1]
    each(1, PLANE, lambda i: rk2(i).start())
    rk2r[s] = rk2s[s]

    turn = hot(iota((CR, CR), 1) == (iota((CR, CR), 0) % 16 // 2) * 32 + (iota((CR, CR), 0) // 16) * 2 + iota((CR, CR), 0) % 2)

    def regroup(q):
        each(1, COL, lambda i: row1(q, i).wait_recv())
        pltpu.make_async_copy(send1.at[q, me], recv1.at[q, me], loc1.at[q]).wait()
        for n in range(4):
            cols = slice(n * 256, (n + 1) * 256)
            rows = recv1[q, :, :, cols].reshape(CR, 256)
            rows = jnp.dot(turn, rows, preferred_element_type=F32).astype(BF16)
            send2[q, :, :, cols] = rows.reshape(PLANE, 16, 256)
        each(1, PLANE, lambda i: row2(q, i).start())
        pltpu.make_async_copy(send2.at[q, s], own.at[q, s], loc2.at[q]).start()

    def to_up(q):
        return pltpu.make_async_remote_copy(
            src_ref=own.at[q], dst_ref=left.at[core, q], send_sem=ssring.at[0, q], recv_sem=rsring.at[0, q],
            device_id=ring_dev(up, core), device_id_type=MESH,
        )

    def to_down(q):
        return pltpu.make_async_remote_copy(
            src_ref=own.at[q], dst_ref=right.at[q], send_sem=ssring.at[1, q], recv_sem=rsring.at[1, q],
            device_id=ring_dev(down, core), device_id_type=MESH,
        )

    def to_sibling(q, k):
        return pltpu.make_async_remote_copy(
            src_ref=own.at[q] if k == 0 else left.at[1, q], dst_ref=left.at[k, q],
            send_sem=ssring.at[2, q], recv_sem=rsring.at[2, q],
            device_id=sibling, device_id_type=MESH,
        )

    def rk_up():
        return pltpu.make_async_remote_copy(
            src_ref=rk_own, dst_ref=rk_left.at[core], send_sem=ssrk.at[0], recv_sem=rsrk.at[0],
            device_id=ring_dev(up, core), device_id_type=MESH,
        )

    def rk_down():
        return pltpu.make_async_remote_copy(
            src_ref=rk_own, dst_ref=rk_right, send_sem=ssrk.at[1], recv_sem=rsrk.at[1],
            device_id=ring_dev(down, core), device_id_type=MESH,
        )

    def rk_sibling(k):
        return pltpu.make_async_remote_copy(
            src_ref=rk_own if k == 0 else rk_left.at[1], dst_ref=rk_left.at[k], send_sem=ssrk.at[2], recv_sem=rsrk.at[2],
            device_id=sibling, device_id_type=MESH,
        )

    def spread_out(q):
        each(1, PLANE, lambda i: row2(q, i).wait_recv())
        pltpu.make_async_copy(send2.at[q, s], own.at[q, s], loc2.at[q]).wait()
        to_up(q).start()
        to_down(q).start()

        @pl.when(core == 0)
        def _():
            to_sibling(q, 0).start()

    regroup(0)

    n_lane = iota((128, SLOTS), 1)
    m_home[...] = hot(iota((128, SLOTS), 0) == (n_lane // CR) * 16 + n_lane % 16)
    each(1, PLANE, lambda i: rk2(i).wait_recv())
    got = jnp.concatenate([rk2r[t] for t in range(PLANE)], axis=0)
    got = pick(got, m_home[...], 2)
    of_chip = (iota((PLANE, SLOTS), 1) % CR) // 16 == iota((PLANE, SLOTS), 0)
    got = jnp.sum(jnp.where(of_chip, got, 0.0), axis=0, keepdims=True)
    rk_own[...] = jnp.where(got > 0.0, got, jnp.nan)
    rk_up().start()
    rk_down().start()

    @pl.when(core == 0)
    def _():
        rk_sibling(0).start()

    regroup(1)
    spread_out(0)
    regroup(2)
    spread_out(1)
    spread_out(2)

    def stand(row):
        return jnp.broadcast_to(row, (128, SLOTS)).T.reshape(CH, CR, 128)

    lr_own[...] = stand(rk_own[...])
    acc_left[...] = jnp.full(acc_left.shape, -1.0, F32)
    acc_right[...] = jnp.full(acc_right.shape, -1.0, F32)

    def tile(rows, lr, other, rr, accs_left, accs_right):
        scores = lax.dot_general(rows, other, dims, preferred_element_type=F32)
        for h in range(2):
            half = scores[:, h * 128 : (h + 1) * 128]
            rank_right = rr[:, h * 128 : (h + 1) * 128]
            low = jnp.where(rank_right < lr, half, -1.0)
            high = jnp.where(rank_right > lr, half, -1.0)
            if accs_left is not None:
                accs_left[0][...] = jnp.maximum(accs_left[0][...], low)
                accs_left[1][...] = jnp.maximum(accs_left[1][...], high)
            cols = slice(h * 128, (h + 1) * 128)
            accs_right[0][:, cols] = jnp.maximum(accs_right[0][:, cols], jnp.max(high.reshape(32, 8, 128), axis=0))
            accs_right[1][:, cols] = jnp.maximum(accs_right[1][:, cols], jnp.max(low.reshape(32, 8, 128), axis=0))

    def lanes(ref, q):
        return ref[:, pl.ds(pl.multiple_of(q * CR, CR), CR)]

    def self_tile(i, c):
        qa, qb = i // CH, i % CH
        tile(
            own[qa].reshape(CR, D), lr_own[qa], own[qb].reshape(CR, D), lanes(rk_own, qb),
            None, (acc_right.at[0, 0, qb], acc_right.at[0, 1, qb]),
        )
        return c

    lax.fori_loop(0, CH * CH, self_tile, 0)

    rk_up().wait_recv()

    @pl.when(core == 1)
    def _():
        rk_sibling(1).start()

    rk_down().wait_recv()
    rk_sibling(0).wait_recv()
    for a in range(2):
        lr_left[a] = stand(rk_left[a])
    n_row, l_col = iota((2 * SLOTS, 128), 0), iota((2 * SLOTS, 128), 1)
    m_back[...] = hot(
        (l_col < 96) & (l_col // 48 == n_row // SLOTS) & ((l_col % 48) // 16 == (n_row % SLOTS) // CR) & (l_col % 16 == n_row % 16)
    )

    def own_tile(a, qa, qb):
        tile(
            left[a, qa].reshape(CR, D), lr_left[a, qa], own[qb].reshape(CR, D), lanes(rk_own, qb),
            (acc_left.at[a, 0, qa], acc_left.at[a, 1, qa]), (acc_right.at[0, 0, qb], acc_right.at[0, 1, qb]),
        )

    def far_tile(a, qa, qb):
        tile(
            left[a, qa].reshape(CR, D), lr_left[a, qa], right[qb].reshape(CR, D), lanes(rk_right, qb),
            (acc_left.at[a, 0, qa], acc_left.at[a, 1, qa]), (acc_right.at[1, 0, qb], acc_right.at[1, 1, qb]),
        )

    for q in range(CH):
        to_up(q).wait_recv()

        @pl.when(core == 1)
        def _():
            to_sibling(q, 1).start()

        to_sibling(q, 0).wait_recv()
        each(0, 2 * CH, lambda i: own_tile(i // CH, q, i % CH))
        to_down(q).wait_recv()
        each(0, 2 * (q + 1), lambda i: far_tile(i // (q + 1), q, i % (q + 1)))
        if q:
            each(0, 2 * q, lambda i: far_tile(i // q, i % q, q))

    def lie(acc):
        return jnp.max(acc.reshape(SLOTS, 128).T, axis=0, keepdims=True)

    def flat(acc):
        return jnp.concatenate([jnp.max(acc[q], axis=0, keepdims=True) for q in range(CH)], axis=1)

    def part(m, to):
        return pltpu.make_async_remote_copy(
            src_ref=part_s.at[m], dst_ref=part_r.at[m], send_sem=sspart.at[m], recv_sem=rspart.at[m],
            device_id=to, device_id_type=MESH,
        )

    to0 = ring_dev(down, core)
    to1 = ring_dev(jnp.where(core == 0, down, s), 1 - core)
    to2 = ring_dev(up, core)
    for el in range(2):
        part_s[2, el : el + 1, :] = flat(acc_right[1, el])
    part(2, to2).start()
    for m in range(2):
        for el in range(2):
            part_s[m, el : el + 1, :] = lie(acc_left[core if m == 0 else 1 - core, el])
        part(m, to0 if m == 0 else to1).start()
    mine = [flat(acc_right[0, el]) for el in range(2)]
    part(2, to2).wait_recv()
    part(0, to0).wait_recv()
    part(1, to1).wait_recv()
    for m in range(3):
        for el in range(2):
            mine[el] = jnp.maximum(mine[el], part_r[m, el : el + 1, :])

    def back1(i):
        t = (s + i) % PLANE
        return pltpu.make_async_remote_copy(
            src_ref=b1s.at[t], dst_ref=b1r.at[s], send_sem=ssb1.at[i], recv_sem=rsb1.at[i],
            device_id=ring_dev(t, core), device_id_type=MESH,
        )

    def back2(i):
        g = (me + i) % COL
        return pltpu.make_async_remote_copy(
            src_ref=b2s.at[g], dst_ref=b2r.at[me], send_sem=ssb2.at[i], recv_sem=rsb2.at[i],
            device_id=col_dev(g), device_id_type=MESH,
        )

    both = jnp.concatenate([jnp.where(of_chip, m, 0.0) for m in mine], axis=1)
    both = pick(both, m_back[...], 3)
    for t in range(PLANE):
        b1s[t] = both[t : t + 1]
    each(1, PLANE, lambda i: back1(i).start())
    b1r[s] = b1s[s]
    a, b = iota((128, 256), 0), iota((128, 256), 1)
    unfold = hot(
        (a // 48 == b // 128) & ((a % 48) // 16 == (b % 128) // 32) & (a % 2 == b % 2) & (b % 128 < 96)
    )
    each(1, PLANE, lambda i: back1(i).wait_recv())
    got = jnp.concatenate([b1r[t] for t in range(PLANE)], axis=0)
    wide = jnp.where((iota((COL, PLANE, 128), 2) % 16) // 2 == iota((COL, PLANE, 128), 0), got[None], 0.0)
    wide = pick(wide.reshape(128, 128), unfold, 3).reshape(COL, PLANE, 256)
    wide = jnp.where((iota((COL, PLANE, 256), 2) % 32) // 2 == iota((COL, PLANE, 256), 1), wide, 0.0)
    wide = jnp.sum(wide, axis=1)
    for g in range(COL):
        b2s[g] = wide[g : g + 1]
    each(1, COL, lambda i: back2(i).start())
    b2r[me] = b2s[me]
    each(1, COL, lambda i: back2(i).wait_recv())
    got = jnp.concatenate([b2r[g] for g in range(COL)], axis=0)
    got = jnp.concatenate([got[:, :128], got[:, 128:]], axis=0)
    got = pick(got, at_spot, 3)
    out_early[...] = jnp.sum(jnp.where(at_goal, got[:COL], 0.0), axis=0, keepdims=True)
    out_late[...] = jnp.sum(jnp.where(at_goal, got[COL:], 0.0), axis=0, keepdims=True)

    each(1, COL, lambda i: rk1(i).wait_send())
    each(1, PLANE, lambda i: rk2(i).wait_send())
    for q in range(CH):
        each(1, COL, lambda i: row1(q, i).wait_send())
        each(1, PLANE, lambda i: row2(q, i).wait_send())
        to_up(q).wait_send()
        to_down(q).wait_send()
        to_sibling(q, 0).wait_send()
    rk_up().wait_send()
    rk_down().wait_send()
    rk_sibling(0).wait_send()
    part(0, to0).wait_send()
    part(1, to1).wait_send()
    part(2, to2).wait_send()
    each(1, PLANE, lambda i: back1(i).wait_send())
    each(1, COL, lambda i: back2(i).wait_send())


def body(embeddings, ranks, routes):
    meta = jnp.stack([routes[:, 0], ranks])
    dma = pltpu.SemaphoreType.DMA
    vm = pltpu.VMEM
    early, late = pl.pallas_call(
        kernel,
        out_shape=[jax.ShapeDtypeStruct((1, ROWS), F32)] * 2,
        in_specs=[pl.BlockSpec(memory_space=vm)] * 2,
        out_specs=[pl.BlockSpec(memory_space=vm)] * 2,
        scratch_shapes=[
            vm((CH, COL, 32, D), BF16),
            vm((CH, COL, 32, D), BF16),
            vm((CH, PLANE, 16, D), BF16),
            vm((CH, PLANE, 16, D), BF16),
            vm((2, CH, PLANE, 16, D), BF16),
            vm((CH, PLANE, 16, D), BF16),
            vm((COL, 1, 128), F32),
            vm((COL, 1, 128), F32),
            vm((PLANE, 1, 128), F32),
            vm((PLANE, 1, 128), F32),
            vm((1, SLOTS), F32),
            vm((2, 1, SLOTS), F32),
            vm((1, SLOTS), F32),
            vm((CH, CR, 128), F32),
            vm((2, CH, CR, 128), F32),
            vm((2, 2, CH, CR, 128), F32),
            vm((2, 2, CH, 8, CR), F32),
            vm((3, 2, SLOTS), F32),
            vm((3, 2, SLOTS), F32),
            vm((PLANE, 1, 128), F32),
            vm((PLANE, 1, 128), F32),
            vm((COL, 1, 256), F32),
            vm((COL, 1, 256), F32),
            vm((128, SLOTS), BF16),
            vm((2 * SLOTS, 128), BF16),
            dma((CH, COL)), dma((CH, COL)),
            dma((CH, PLANE)), dma((CH, PLANE)),
            dma((COL,)), dma((COL,)),
            dma((PLANE,)), dma((PLANE,)),
            dma((3, CH)), dma((3, CH)),
            dma((3,)), dma((3,)),
            dma((3,)), dma((3,)),
            dma((PLANE,)), dma((PLANE,)),
            dma((COL,)), dma((COL,)),
            dma((CH,)), dma((CH,)),
        ],
        compiler_params=pltpu.CompilerParams(
            collective_id=0, has_side_effects=True, vmem_limit_bytes=48 * 2**20
        ),
    )(embeddings, meta)
    return early.reshape(ROWS), late.reshape(ROWS)


def solution(mesh):
    placed = (P(("group", "blk"), None), P(("group", "blk")), P(("group", "blk"), None))
    return jax.shard_map(
        body,
        mesh=mesh,
        in_specs=placed,
        out_specs=(P(("group", "blk")), P(("group", "blk"))),
        check_vma=False,
    )
```

```python
import jax
import jax.numpy as jnp
from jax import lax
from jax.experimental import pallas as pl
from jax.experimental.pallas import tpu as pltpu
from jax.sharding import PartitionSpec as P

MESH = pl.DeviceIdType.MESH
F32 = jnp.float32
BF16 = jnp.bfloat16

D = 1024
HALF = 512
ROWS = 384
SLOTS = 768
CH = 3
CR = 256
COL = 8
PLANE = 16

RINGS = (
    (0, 4, 8, 12, 13, 1, 5, 9, 10, 14, 2, 6, 7, 11, 15, 3),
    (0, 1, 2, 3, 7, 4, 5, 6, 10, 11, 8, 9, 13, 14, 15, 12),
)
PLACES = tuple(tuple(r.index(n) for n in range(PLANE)) for r in RINGS)
UPS = tuple(tuple(r[(r.index(n) + 1) % PLANE] for n in range(PLANE)) for r in RINGS)
DOWNS = tuple(tuple(r[(r.index(n) - 1) % PLANE] for n in range(PLANE)) for r in RINGS)
STRAIGHT = 11
DETOURS = ((0, 1, 11, 14), (0, -1, 14, 16), (1, -1, 11, 14), (1, 1, 14, 16))


def iota(shape, dim):
    return lax.broadcasted_iota(jnp.int32, shape, dim)


def hot(mask):
    return jnp.where(mask, 1.0, 0.0).astype(BF16)


def pick(x, onehot, parts):
    rows = x.shape[0]
    pieces = []
    for _ in range(parts):
        piece = x.astype(BF16)
        pieces.append(piece)
        x = x - piece.astype(F32)
    out = jnp.dot(jnp.concatenate(pieces, axis=0), onehot, preferred_element_type=F32)
    total = out[(parts - 1) * rows :]
    for p in range(parts - 2, -1, -1):
        total = total + out[p * rows : (p + 1) * rows]
    return total


def look(tables, odd, index):
    found = index * 0
    for i in range(PLANE):
        found = jnp.where(index == i, jnp.where(odd == 1, tables[1][i], tables[0][i]), found)
    return found


def device(n, z, core):
    x, y = n // 4, n % 4
    return ((y % 2) * 2 + core, (y // 2) * 16 + x * 4 + z)


def each(first, last, act):
    def step(i, c):
        act(i)
        return c

    lax.fori_loop(first, last, step, 0)


def kernel(
    emb_hbm, ranks, routes, out_early, out_late,
    emb, send1a, recv1a, send2a, send1b, recv1b, send2b, recv2b, own, left, right, relay,
    rk1s, rk1r, rk2s, rk2r, rk_own, rk_left, rk_right,
    lr_own, lr_left, acc_left, acc_right,
    b1s, b1r, b2s, b2r, m_home, m_back,
    ss1a, rs1a, ss2a, rs2a, ss1b, rs1b, ss2b, rs2b, ssr1, rsr1, ssr2, rsr2,
    ssring, rsring, ssleg1, rsleg1, ssleg2, rsleg2, ssrk, rsrk,
    ssb1, rsb1, ssb2, rsb2, loc, emb_sem,
):
    load = pltpu.make_async_copy(emb_hbm, emb, emb_sem)
    load.start()
    grp = lax.axis_index("group")
    blk = lax.axis_index("blk")
    z, core = blk % 4, grp % 2
    n = ((blk // 4) % 4) * 4 + (blk // 16) * 2 + grp // 2
    me = core * 4 + z
    odd = z % 2
    s = look(PLACES, odd, n)
    up, down = look(UPS, odd, n), look(DOWNS, odd, n)
    beside = (look(UPS, 1 - odd, n), look(DOWNS, 1 - odd, n))

    def col_dev(g):
        return device(n, g % 4, g // 4)

    def plane_dev(t):
        return device(t, z, core)

    sibling = device(n, z, 1 - core)

    barrier = pltpu.get_barrier_semaphore()

    def greet(to):
        pl.semaphore_signal(barrier, inc=1, device_id=to, device_id_type=MESH)

    each(1, COL, lambda i: greet(col_dev((me + i) % COL)))
    each(1, PLANE, lambda i: greet(plane_dev((n + i) % PLANE)))
    for way, side, _, _ in DETOURS:
        greet(device(down if way == 0 else up, (z + side) % 4, core))

    target = routes[...].reshape(1, ROWS)
    rank = ranks[...].reshape(1, ROWS).astype(F32) + 1.0
    spread = iota((128, ROWS), 0) == target
    before = hot(iota((ROWS, ROWS), 0) < iota((ROWS, ROWS), 1))
    count = jnp.dot(hot(spread), before, preferred_element_type=F32)
    slot = jnp.sum(jnp.where(spread, count, 0.0), axis=0, keepdims=True).astype(jnp.int32)
    cluster, block = target // 32, target % 32
    goal = (block % 2) * 4 + cluster
    ring = block // 2
    to_chip = look(RINGS, cluster % 2, ring)
    chunk, two = slot // 2, slot % 2
    at_goal = iota((COL, ROWS), 0) == goal
    at_spot = hot(iota((128, ROWS), 0) == chunk * 32 + to_chip * 2 + two)
    at_back = hot(iota((128, ROWS), 0) == chunk * 32 + ring * 2 + two)
    ranks16 = jnp.concatenate([jnp.where(at_goal, rank, 0.0), jnp.zeros((COL, ROWS), F32)], axis=0)
    hi = ranks16.astype(BF16)
    lo = (ranks16 - hi.astype(F32)).astype(BF16)
    dims = (((1,), (1,)), ((), ()))
    packed = lax.dot_general(hi, at_spot, dims, preferred_element_type=F32) + lax.dot_general(
        lo, at_spot, dims, preferred_element_type=F32
    )
    for g in range(COL):
        rk1s[g] = packed[g : g + 1]
    load.wait()
    e = emb[...]
    mean_square = jnp.mean(e * e, axis=-1, keepdims=True)
    unit = (e * lax.rsqrt(mean_square + 1e-06) * D ** (-0.5)).astype(BF16)

    def fill(q):
        for index, ref, first, shape in (
            (goal * 32 + to_chip * 2 + two, send1a, 0, (COL, 32, 256)),
            (to_chip * 16 + goal * 2 + two, send1b, HALF, (PLANE, 16, 256)),
        ):
            select = hot(iota((CR, ROWS), 0) == jnp.where(chunk == q, index, -1))
            for c in range(0, HALF, 256):
                rows = jnp.dot(select, unit[:, first + c : first + c + 256], preferred_element_type=F32)
                ref[q, :, :, c : c + 256] = rows.astype(BF16).reshape(shape)

    def copy(src, dst, send, recv, to):
        return pltpu.make_async_remote_copy(
            src_ref=src, dst_ref=dst, send_sem=send, recv_sem=recv, device_id=to, device_id_type=MESH
        )

    def rk1(i):
        g = (me + i) % COL
        return copy(rk1s.at[g], rk1r.at[me], ssr1.at[i], rsr1.at[i], col_dev(g))

    def rk2(i):
        t = (n + i) % PLANE
        return copy(rk2s.at[t], rk2r.at[n], ssr2.at[i], rsr2.at[i], plane_dev(t))

    def row1a(q, i):
        g = (me + i) % COL
        return copy(send1a.at[q, g], recv1a.at[q, me], ss1a.at[q, i], rs1a.at[q, i], col_dev(g))

    def row2a(q, i):
        t = (n + i) % PLANE
        return copy(send2a.at[q, t], own.at[q, n, :, pl.ds(0, HALF)], ss2a.at[q, i], rs2a.at[q, i], plane_dev(t))

    def row1b(q, i):
        t = (n + i) % PLANE
        return copy(send1b.at[q, t], recv1b.at[q, n], ss1b.at[q, i], rs1b.at[q, i], plane_dev(t))

    def row2b(q, i):
        g = (me + i) % COL
        return copy(send2b.at[q, g], recv2b.at[q, me], ss2b.at[q, i], rs2b.at[q, i], col_dev(g))

    def stay1a(q):
        return pltpu.make_async_copy(send1a.at[q, me], recv1a.at[q, me], loc.at[0, q])

    def stay2a(q):
        return pltpu.make_async_copy(send2a.at[q, n], own.at[q, n, :, pl.ds(0, HALF)], loc.at[1, q])

    def stay1b(q):
        return pltpu.make_async_copy(send1b.at[q, n], recv1b.at[q, n], loc.at[2, q])

    def stay2b(q):
        return pltpu.make_async_copy(send2b.at[q, me], recv2b.at[q, me], loc.at[3, q])

    fill(0)
    pl.semaphore_wait(barrier, COL - 1 + PLANE - 1 + len(DETOURS))
    each(1, COL, lambda i: rk1(i).start())
    for q in range(CH):
        if q:
            fill(q)
        each(1, COL, lambda i: row1a(q, i).start())
        each(1, PLANE, lambda i: row1b(q, i).start())
        stay1a(q).start()
        stay1b(q).start()

    rk1r[me] = rk1s[me]
    each(1, COL, lambda i: rk1(i).wait_recv())
    seen = jnp.concatenate([rk1r[g] for g in range(COL)], axis=0)
    lane = iota((PLANE, COL, 128), 2)
    wide = jnp.where((lane % 32) // 2 == iota((PLANE, COL, 128), 0), seen[None], 0.0)
    a, b = iota((128, 128), 0), iota((128, 128), 1)
    fold = hot((a // 32 == b // 16) & (a % 2 == b % 2) & (a < 96) & (b < 48))
    wide = pick(wide.reshape(128, 128), fold, 2).reshape(PLANE, COL, 128)
    wide = jnp.sum(jnp.where((lane % 16) // 2 == iota((PLANE, COL, 128), 1), wide, 0.0), axis=1)
    for t in range(PLANE):
        rk2s[t] = wide[t : t + 1]
    each(1, PLANE, lambda i: rk2(i).start())
    rk2r[n] = rk2s[n]

    a, b = iota((CR, CR), 0), iota((CR, CR), 1)
    by_chip = hot(b == (a % 16 // 2) * 32 + (a // 16) * 2 + a % 2)
    by_goal = hot(b == (a % 32 // 2) * 16 + (a // 32) * 2 + a % 2)

    def turn(order, src, dst, q, first, shape):
        for c in range(0, HALF, 256):
            rows = jnp.dot(order, src[q, :, :, c : c + 256].reshape(CR, 256), preferred_element_type=F32)
            dst[q, :, :, first + c : first + c + 256] = rows.astype(BF16).reshape(shape)

    def regroup(q):
        each(1, COL, lambda i: row1a(q, i).wait_recv())
        stay1a(q).wait()
        turn(by_chip, recv1a, send2a, q, 0, (PLANE, 16, 256))
        each(1, PLANE, lambda i: row2a(q, i).start())
        stay2a(q).start()
        each(1, PLANE, lambda i: row1b(q, i).wait_recv())
        stay1b(q).wait()
        turn(by_goal, recv1b, send2b, q, 0, (COL, 32, 256))
        each(1, COL, lambda i: row2b(q, i).start())
        stay2b(q).start()

    def straight(way, q):
        rows = pl.ds(0, STRAIGHT)
        return copy(
            own.at[q, rows], left.at[core, q, rows] if way == 0 else right.at[q, rows],
            ssring.at[way, q], rsring.at[way, q], plane_dev(up if way == 0 else down),
        )

    def leg1(d, q):
        _, side, first, last = DETOURS[d]
        return copy(
            own.at[q, pl.ds(first, last - first)], relay.at[d, q, pl.ds(0, last - first)],
            ssleg1.at[d, q], rsleg1.at[d, q], device(n, (z + side) % 4, core),
        )

    def leg2(d, q):
        way, side, first, last = DETOURS[d]
        rows = pl.ds(first, last - first)
        return copy(
            relay.at[d, q, pl.ds(0, last - first)], left.at[core, q, rows] if way == 0 else right.at[q, rows],
            ssleg2.at[d, q], rsleg2.at[d, q], device(beside[way], (z - side) % 4, core),
        )

    def to_sibling(q, k):
        return copy(own.at[q] if k == 0 else left.at[1, q], left.at[k, q], ssring.at[2, q], rsring.at[2, q], sibling)

    def rk_ring(way):
        return copy(
            rk_own, rk_left.at[core] if way == 0 else rk_right,
            ssrk.at[way], rsrk.at[way], plane_dev(up if way == 0 else down),
        )

    def rk_sibling(k):
        return copy(rk_own if k == 0 else rk_left.at[1], rk_left.at[k], ssrk.at[2], rsrk.at[2], sibling)

    def spread_out(q):
        each(1, COL, lambda i: row2b(q, i).wait_recv())
        stay2b(q).wait()
        turn(by_chip, recv2b, own, q, HALF, (PLANE, 16, 256))
        each(1, PLANE, lambda i: row2a(q, i).wait_recv())
        stay2a(q).wait()
        for d in range(len(DETOURS)):
            leg1(d, q).start()
        straight(0, q).start()
        straight(1, q).start()

        @pl.when(core == 0)
        def _():
            to_sibling(q, 0).start()

    def pass_on(q):
        for d in range(len(DETOURS)):
            leg1(d, q).wait_recv()
            leg2(d, q).start()

    regroup(0)

    n_lane = iota((128, SLOTS), 1)
    m_home[...] = hot(iota((128, SLOTS), 0) == (n_lane // CR) * 16 + n_lane % 16)
    each(1, PLANE, lambda i: rk2(i).wait_recv())
    got = jnp.concatenate([rk2r[t] for t in range(PLANE)], axis=0)
    got = pick(got, m_home[...], 2)
    of_chip = (iota((PLANE, SLOTS), 1) % CR) // 16 == iota((PLANE, SLOTS), 0)
    got = jnp.sum(jnp.where(of_chip, got, 0.0), axis=0, keepdims=True)
    rk_own[...] = jnp.where(got > 0.0, got, jnp.nan)
    rk_ring(0).start()
    rk_ring(1).start()

    @pl.when(core == 0)
    def _():
        rk_sibling(0).start()

    regroup(1)
    spread_out(0)
    regroup(2)
    spread_out(1)
    pass_on(0)
    spread_out(2)
    pass_on(1)

    def stand(row):
        return jnp.broadcast_to(row, (128, SLOTS)).T.reshape(CH, CR, 128)

    lr_own[...] = stand(rk_own[...])
    acc_left[...] = jnp.full(acc_left.shape, -1.0, F32)
    acc_right[...] = jnp.full(acc_right.shape, -1.0, F32)

    def tile(rows, lr, other, rr, accs_left, accs_right):
        scores = lax.dot_general(rows, other, dims, preferred_element_type=F32)
        for h in range(2):
            half = scores[:, h * 128 : (h + 1) * 128]
            rank_right = rr[:, h * 128 : (h + 1) * 128]
            low = jnp.where(rank_right < lr, half, -1.0)
            high = jnp.where(rank_right > lr, half, -1.0)
            if accs_left is not None:
                accs_left[0][...] = jnp.maximum(accs_left[0][...], low)
                accs_left[1][...] = jnp.maximum(accs_left[1][...], high)
            cols = slice(h * 128, (h + 1) * 128)
            accs_right[0][:, cols] = jnp.maximum(accs_right[0][:, cols], jnp.max(high.reshape(32, 8, 128), axis=0))
            accs_right[1][:, cols] = jnp.maximum(accs_right[1][:, cols], jnp.max(low.reshape(32, 8, 128), axis=0))

    def lanes(ref, q):
        return ref[:, pl.ds(pl.multiple_of(q * CR, CR), CR)]

    def self_tile(i):
        qa, qb = i // CH, i % CH
        tile(
            own[qa].reshape(CR, D), lr_own[qa], own[qb].reshape(CR, D), lanes(rk_own, qb),
            None, (acc_right.at[0, 0, qb], acc_right.at[0, 1, qb]),
        )

    each(0, CH * CH, self_tile)
    pass_on(2)

    rk_ring(0).wait_recv()

    @pl.when(core == 1)
    def _():
        rk_sibling(1).start()

    rk_ring(1).wait_recv()
    rk_sibling(0).wait_recv()
    for a in range(2):
        lr_left[a] = stand(rk_left[a])
    n_row, l_col = iota((2 * SLOTS, 128), 0), iota((2 * SLOTS, 128), 1)
    m_back[...] = hot(
        (l_col < 96) & (l_col // 48 == n_row // SLOTS) & ((l_col % 48) // 16 == (n_row % SLOTS) // CR) & (l_col % 16 == n_row % 16)
    )

    def own_tile(a, qa, qb):
        tile(
            left[a, qa].reshape(CR, D), lr_left[a, qa], own[qb].reshape(CR, D), lanes(rk_own, qb),
            (acc_left.at[a, 0, qa], acc_left.at[a, 1, qa]), (acc_right.at[0, 0, qb], acc_right.at[0, 1, qb]),
        )

    def far_tile(a, qa, qb):
        tile(
            left[a, qa].reshape(CR, D), lr_left[a, qa], right[qb].reshape(CR, D), lanes(rk_right, qb),
            (acc_left.at[a, 0, qa], acc_left.at[a, 1, qa]), (acc_right.at[1, 0, qb], acc_right.at[1, 1, qb]),
        )

    def arrived(way, q):
        straight(way, q).wait_recv()
        for d, detour in enumerate(DETOURS):
            if detour[0] == way:
                leg2(d, q).wait_recv()

    for q in range(CH):
        arrived(0, q)

        @pl.when(core == 1)
        def _():
            to_sibling(q, 1).start()

        to_sibling(q, 0).wait_recv()
        each(0, 2 * CH, lambda i: own_tile(i // CH, q, i % CH))
        arrived(1, q)
        each(0, 2 * (q + 1), lambda i: far_tile(i // (q + 1), q, i % (q + 1)))
        if q:
            each(0, 2 * q, lambda i: far_tile(i // q, i % q, q))

    def back1(i):
        t = (n + i) % PLANE
        return copy(b1s.at[t], b1r.at[s], ssb1.at[i], rsb1.at[i], plane_dev(t))

    def back2(i):
        g = (me + i) % COL
        return copy(b2s.at[g], b2r.at[me], ssb2.at[i], rsb2.at[i], col_dev(g))

    def lie(acc):
        return jnp.max(acc.reshape(SLOTS, 128).T, axis=0, keepdims=True)

    def flat(acc):
        return jnp.concatenate([jnp.max(acc[q], axis=0, keepdims=True) for q in range(CH)], axis=1)

    found = [[lie(acc_left[a, el]) for el in range(2)] for a in range(2)]
    found += [[flat(acc_right[r, el]) for el in range(2)] for r in range(2)]
    found = [jnp.concatenate([jnp.where(of_chip, m, 0.0) for m in f], axis=1) for f in found]
    found = pick(jnp.concatenate(found, axis=0), m_back[...], 3)
    for t in range(PLANE):
        for k in range(4):
            b1s[t, k : k + 1] = found[k * PLANE + t : k * PLANE + t + 1]
    each(1, PLANE, lambda i: back1(i).start())
    b1r[s] = b1s[n]
    a, b = iota((128, 256), 0), iota((128, 256), 1)
    unfold = hot((a // 48 == b // 128) & ((a % 48) // 16 == (b % 128) // 32) & (a % 2 == b % 2) & (b % 128 < 96))
    each(1, PLANE, lambda i: back1(i).wait_recv())

    def of(k):
        return jnp.concatenate([b1r[t, k : k + 1] for t in range(PLANE)], axis=0)

    def above(m):
        return jnp.concatenate([m[1:], m[:1]], axis=0)

    def below(m):
        return jnp.concatenate([m[PLANE - 1 :], m[: PLANE - 1]], axis=0)

    left0, left1, right0, right1 = of(0), above(of(1)), of(2), below(of(3))
    even = jnp.where(core == 0, jnp.maximum(jnp.maximum(right0, above(left0)), right1), left0)
    uneven = jnp.where(core == 0, left1, jnp.maximum(jnp.maximum(right0, left1), right1))
    wide = jnp.stack([even, uneven])[:, None]
    shape = (2, COL, PLANE, 128)
    wide = jnp.where((iota(shape, 3) % 16) // 2 == iota(shape, 1), wide, 0.0)
    wide = pick(wide.reshape(2 * COL * PLANE, 128), unfold, 3).reshape(2, COL, PLANE, 256)
    shape = (2, COL, PLANE, 256)
    wide = jnp.sum(jnp.where((iota(shape, 3) % 32) // 2 == iota(shape, 2), wide, 0.0), axis=2)
    wide = jnp.concatenate([wide[0], wide[1]], axis=1)
    for g in range(COL):
        b2s[g] = wide[g : g + 1]
    each(1, COL, lambda i: back2(i).start())
    b2r[me] = b2s[me]
    each(1, COL, lambda i: back2(i).wait_recv())
    got = jnp.concatenate([b2r[g] for g in range(COL)], axis=0)
    got = jnp.maximum(got[:4], got[4:])
    got = jnp.concatenate([got[:, c : c + 128] for c in (0, 256, 128, 384)], axis=0)
    got = pick(got, at_back, 3)
    out_early[...] = jnp.sum(jnp.where(at_goal, got[:COL], 0.0), axis=0)
    out_late[...] = jnp.sum(jnp.where(at_goal, got[COL:], 0.0), axis=0)

    each(1, COL, lambda i: rk1(i).wait_send())
    each(1, PLANE, lambda i: rk2(i).wait_send())
    for q in range(CH):
        each(1, COL, lambda i: row1a(q, i).wait_send())
        each(1, PLANE, lambda i: row2a(q, i).wait_send())
        each(1, PLANE, lambda i: row1b(q, i).wait_send())
        each(1, COL, lambda i: row2b(q, i).wait_send())
        straight(0, q).wait_send()
        straight(1, q).wait_send()
        for d in range(len(DETOURS)):
            leg1(d, q).wait_send()
            leg2(d, q).wait_send()
        to_sibling(q, 0).wait_send()
    rk_ring(0).wait_send()
    rk_ring(1).wait_send()
    rk_sibling(0).wait_send()
    each(1, PLANE, lambda i: back1(i).wait_send())
    each(1, COL, lambda i: back2(i).wait_send())


def body(embeddings, ranks, routes):
    dma = pltpu.SemaphoreType.DMA
    vm = pltpu.VMEM
    here = pl.BlockSpec(memory_space=vm)
    return tuple(pl.pallas_call(
        kernel,
        out_shape=[jax.ShapeDtypeStruct((ROWS,), F32)] * 2,
        in_specs=[pl.BlockSpec(memory_space=pltpu.HBM), here, here],
        out_specs=[here] * 2,
        scratch_shapes=[
            vm((ROWS, D), F32),
            vm((CH, COL, 32, HALF), BF16),
            vm((CH, COL, 32, HALF), BF16),
            vm((CH, PLANE, 16, HALF), BF16),
            vm((CH, PLANE, 16, HALF), BF16),
            vm((CH, PLANE, 16, HALF), BF16),
            vm((CH, COL, 32, HALF), BF16),
            vm((CH, COL, 32, HALF), BF16),
            vm((CH, PLANE, 16, D), BF16),
            vm((2, CH, PLANE, 16, D), BF16),
            vm((CH, PLANE, 16, D), BF16),
            vm((4, CH, 3, 16, D), BF16),
            vm((COL, 1, 128), F32),
            vm((COL, 1, 128), F32),
            vm((PLANE, 1, 128), F32),
            vm((PLANE, 1, 128), F32),
            vm((1, SLOTS), F32),
            vm((2, 1, SLOTS), F32),
            vm((1, SLOTS), F32),
            vm((CH, CR, 128), F32),
            vm((2, CH, CR, 128), F32),
            vm((2, 2, CH, CR, 128), F32),
            vm((2, 2, CH, 8, CR), F32),
            vm((PLANE, 4, 128), F32),
            vm((PLANE, 4, 128), F32),
            vm((COL, 1, 512), F32),
            vm((COL, 1, 512), F32),
            vm((128, SLOTS), BF16),
            vm((2 * SLOTS, 128), BF16),
            dma((CH, COL)), dma((CH, COL)),
            dma((CH, PLANE)), dma((CH, PLANE)),
            dma((CH, PLANE)), dma((CH, PLANE)),
            dma((CH, COL)), dma((CH, COL)),
            dma((COL,)), dma((COL,)),
            dma((PLANE,)), dma((PLANE,)),
            dma((3, CH)), dma((3, CH)),
            dma((4, CH)), dma((4, CH)),
            dma((4, CH)), dma((4, CH)),
            dma((3,)), dma((3,)),
            dma((PLANE,)), dma((PLANE,)),
            dma((COL,)), dma((COL,)),
            dma((4, CH)), dma,
        ],
        compiler_params=pltpu.CompilerParams(
            collective_id=0, has_side_effects=True, vmem_limit_bytes=48 * 2**20
        ),
    )(embeddings, ranks, routes.reshape(ROWS)))


def solution(mesh):
    placed = (P(("group", "blk"), None), P(("group", "blk")), P(("group", "blk"), None))
    return jax.shard_map(
        body,
        mesh=mesh,
        in_specs=placed,
        out_specs=(P(("group", "blk")), P(("group", "blk"))),
        check_vma=False,
    )
```

```python
import jax
import jax.numpy as jnp
from jax import lax
from jax.experimental import pallas as pl
from jax.experimental.pallas import tpu as pltpu
from jax.sharding import PartitionSpec as P

MESH = pl.DeviceIdType.MESH
F32 = jnp.float32
BF16 = jnp.bfloat16

D = 1024
VMEM_LIMIT = 62 * 2**20
HALF = 512
ROWS = 384
SLOTS = 768
CH = 3
CR = 256
COL = 8
PLANE = 16

RINGS = (
    (0, 4, 8, 12, 13, 1, 5, 9, 10, 14, 2, 6, 7, 11, 15, 3),
    (0, 1, 2, 3, 7, 4, 5, 6, 10, 11, 8, 9, 13, 14, 15, 12),
)
PLACES = tuple(tuple(r.index(n) for n in range(PLANE)) for r in RINGS)
UPS = tuple(tuple(r[(r.index(n) + 1) % PLANE] for n in range(PLANE)) for r in RINGS)
DOWNS = tuple(tuple(r[(r.index(n) - 1) % PLANE] for n in range(PLANE)) for r in RINGS)
STRAIGHT = 11
DETOURS = ((0, 1, 11, 14), (0, -1, 14, 16), (1, -1, 11, 14), (1, 1, 14, 16))


def iota(shape, dim):
    return lax.broadcasted_iota(jnp.int32, shape, dim)


def hot(mask):
    return jnp.where(mask, 1.0, 0.0).astype(BF16)


def pick(x, onehot, parts):
    rows = x.shape[0]
    pieces = []
    for _ in range(parts):
        piece = x.astype(BF16)
        pieces.append(piece)
        x = x - piece.astype(F32)
    out = jnp.dot(jnp.concatenate(pieces, axis=0), onehot, preferred_element_type=F32)
    total = out[(parts - 1) * rows :]
    for p in range(parts - 2, -1, -1):
        total = total + out[p * rows : (p + 1) * rows]
    return total


def look(tables, odd, index):
    found = index * 0
    for i in range(PLANE):
        found = jnp.where(index == i, jnp.where(odd == 1, tables[1][i], tables[0][i]), found)
    return found


def rem(a, b):
    return lax.rem(a, b)


def device(n, z, core):
    x, y = lax.div(n, 4), rem(n, 4)
    return (rem(y, 2) * 2 + core, lax.div(y, 2) * 16 + x * 4 + z)


def each(first, last, act):
    def step(i, c):
        act(i)
        return c

    lax.fori_loop(first, last, step, 0)


def kernel(
    emb_hbm, ranks_hbm, routes_hbm, out_early, out_late,
    emb, ranks, routes, send1a, recv1a, send2a, send1b, recv1b, send2b, recv2b, own, left, right, relay,
    rk1s, rk1r, rk2s, rk2r, rk_own, rk_left, rk_right,
    lr_own, lr_left, acc_left, acc_right,
    b1s, b1r, b2s, b2r, by_chip, by_goal, m_home, m_back, unfold,
    ss_row, rs1a, rs2a, rs1b, rs2b, ss_rank, rs_rank,
    ss_ring, rs_ring, ss_leg1, rs_leg1, ss_leg2, ss_back, rs_back, loc, in_sem,
):
    loads = [
        pltpu.make_async_copy(src, dst, in_sem.at[i])
        for i, (src, dst) in enumerate(((routes_hbm, routes), (ranks_hbm, ranks), (emb_hbm, emb)))
    ]
    for load in loads:
        load.start()
    grp = lax.axis_index("group")
    blk = lax.axis_index("blk")
    z, core = rem(blk, 4), rem(grp, 2)
    n = rem(lax.div(blk, 4), 4) * 4 + lax.div(blk, 16) * 2 + lax.div(grp, 2)
    me = core * 4 + z
    odd = rem(z, 2)

    def col_dev(g):
        return device(n, rem(g, 4), lax.div(g, 4))

    def plane_dev(t):
        return device(t, z, core)

    sibling = device(n, z, 1 - core)

    barrier = pltpu.get_barrier_semaphore()

    def greet(to):
        pl.semaphore_signal(barrier, inc=1, device_id=to, device_id_type=MESH)

    each(1, PLANE, lambda i: greet(plane_dev(rem(n + i, PLANE))))
    each(1, COL, lambda i: greet(col_dev(rem(me + i, COL))))
    s = look(PLACES, odd, n)
    up, down = look(UPS, odd, n), look(DOWNS, odd, n)
    beside = (look(UPS, 1 - odd, n), look(DOWNS, 1 - odd, n))
    for way, side, _, _ in DETOURS:
        greet(device(down if way == 0 else up, rem(z + 4 + side, 4), core))

    loads[0].wait()
    loads[1].wait()
    target = routes[...].reshape(1, ROWS)
    rank = ranks[...].reshape(1, ROWS).astype(F32) + 1.0
    spread = iota((128, ROWS), 0) == target
    before = hot(iota((ROWS, ROWS), 0) < iota((ROWS, ROWS), 1))
    count = jnp.dot(hot(spread), before, preferred_element_type=F32)
    slot = jnp.sum(jnp.where(spread, count, 0.0), axis=0, keepdims=True).astype(jnp.int32)
    cluster, block = target >> 5, target & 31
    goal = (block & 1) * 4 + cluster
    ring = block >> 1
    to_chip = look(RINGS, cluster & 1, ring)
    chunk, two = slot >> 1, slot & 1
    at_goal = iota((COL, ROWS), 0) == goal
    at_spot = hot(iota((128, ROWS), 0) == chunk * 32 + to_chip * 2 + two)
    at_back = hot(iota((128, ROWS), 0) == chunk * 32 + ring * 2 + two)
    ranks16 = jnp.concatenate([jnp.where(at_goal, rank, 0.0), jnp.zeros((COL, ROWS), F32)], axis=0)
    hi = ranks16.astype(BF16)
    lo = (ranks16 - hi.astype(F32)).astype(BF16)
    dims = (((1,), (1,)), ((), ()))
    packed = lax.dot_general(hi, at_spot, dims, preferred_element_type=F32) + lax.dot_general(
        lo, at_spot, dims, preferred_element_type=F32
    )
    for g in range(COL):
        rk1s[g] = packed[g : g + 1]
    loads[2].wait()
    e = emb[...]
    mean_square = jnp.mean(e * e, axis=-1, keepdims=True)
    unit = (e * lax.rsqrt(mean_square + 1e-06) * D ** (-0.5)).astype(BF16)

    def fill(q):
        for index, ref, first, shape in (
            (goal * 32 + to_chip * 2 + two, send1a, 0, (COL, 32, 256)),
            (to_chip * 16 + goal * 2 + two, send1b, HALF, (PLANE, 16, 256)),
        ):
            select = hot(iota((CR, ROWS), 0) == jnp.where(chunk == q, index, -1))
            for c in range(0, HALF, 256):
                rows = jnp.dot(select, unit[:, first + c : first + c + 256], preferred_element_type=F32)
                ref[q, :, :, c : c + 256] = rows.astype(BF16).reshape(shape)

    def copy(src, dst, send, recv, to):
        return pltpu.make_async_remote_copy(
            src_ref=src, dst_ref=dst, send_sem=send, recv_sem=recv, device_id=to, device_id_type=MESH
        )

    def rk1(i):
        g = rem(me + i, COL)
        return copy(rk1s.at[g], rk1r.at[me], ss_rank.at[0], rs_rank.at[0], col_dev(g))

    def rk2(i):
        t = rem(n + i, PLANE)
        return copy(rk2s.at[t], rk2r.at[n], ss_rank.at[1], rs_rank.at[1], plane_dev(t))

    def row1a(q, i):
        g = rem(me + i, COL)
        return copy(send1a.at[q, g], recv1a.at[q, me], ss_row.at[0], rs1a.at[q], col_dev(g))

    def row2a(q, i):
        t = rem(n + i, PLANE)
        return copy(send2a.at[q, t], own.at[q, n, :, pl.ds(0, HALF)], ss_row.at[1], rs2a.at[q], plane_dev(t))

    def row1b(q, i):
        t = rem(n + i, PLANE)
        return copy(send1b.at[q, t], recv1b.at[q, n], ss_row.at[2], rs1b.at[q], plane_dev(t))

    def row2b(q, i):
        g = rem(me + i, COL)
        return copy(send2b.at[q, g], recv2b.at[q, me], ss_row.at[3], rs2b.at[q], col_dev(g))

    def got_all(ref, sem):
        copy(ref, ref, ss_row.at[0], sem, sibling).wait_recv()

    def sent_all(ref, sem):
        copy(ref, ref, sem, rs_rank.at[0], sibling).wait_send()

    def stay1a(q):
        return pltpu.make_async_copy(send1a.at[q, me], recv1a.at[q, me], loc.at[0, q])

    def stay2a(q):
        return pltpu.make_async_copy(send2a.at[q, n], own.at[q, n, :, pl.ds(0, HALF)], loc.at[1, q])

    def stay1b(q):
        return pltpu.make_async_copy(send1b.at[q, n], recv1b.at[q, n], loc.at[2, q])

    def stay2b(q):
        return pltpu.make_async_copy(send2b.at[q, me], recv2b.at[q, me], loc.at[3, q])

    for q in range(CH):
        fill(q)

    a, b = iota((CR, CR), 0), iota((CR, CR), 1)
    by_chip[...] = hot(b == ((a & 15) >> 1) * 32 + (a >> 4) * 2 + (a & 1))
    by_goal[...] = hot(b == ((a & 31) >> 1) * 16 + (a >> 5) * 2 + (a & 1))
    lane = iota((128, SLOTS), 1)
    m_home[...] = hot(iota((128, SLOTS), 0) == (lane >> 8) * 16 + (lane & 15))
    lane = iota((CR, 128), 1)
    same = (lane & 15) == (iota((CR, 128), 0) & 15)
    for i in range(2 * CH):
        m_back[i * CR : (i + 1) * CR] = hot(same & (lane >> 4 == i))
    a, b = iota((128, 256), 0), iota((128, 256), 1)
    unfold[...] = hot(
        (a >> 4 == (b >> 7) * 3 + ((b & 127) >> 5)) & ((a & 1) == (b & 1)) & ((b & 127) < 96)
    )
    acc_left[...] = jnp.full(acc_left.shape, -1.0, F32)
    acc_right[...] = jnp.full(acc_right.shape, -1.0, F32)
    of_chip = ((iota((PLANE, SLOTS), 1) & 255) >> 4) == iota((PLANE, SLOTS), 0)

    pl.semaphore_wait(barrier, COL - 1 + PLANE - 1 + len(DETOURS))
    each(1, COL, lambda i: rk1(i).start())
    for q in range(CH):
        each(1, COL, lambda i: row1a(q, i).start())
        each(1, PLANE, lambda i: row1b(q, i).start())
        stay1a(q).start()
        stay1b(q).start()

    rk1r[me] = rk1s[me]
    got_all(rk1r.at[pl.ds(0, COL - 1)], rs_rank.at[0])
    seen = jnp.concatenate([rk1r[g] for g in range(COL)], axis=0)
    lane = iota((PLANE, COL, 128), 2)
    wide = jnp.where(((lane & 31) >> 1) == iota((PLANE, COL, 128), 0), seen[None], 0.0)
    a, b = iota((128, 128), 0), iota((128, 128), 1)
    fold = hot((a >> 5 == b >> 4) & ((a & 1) == (b & 1)) & (a < 96))
    wide = pick(wide.reshape(128, 128), fold, 2).reshape(PLANE, COL, 128)
    wide = jnp.sum(jnp.where(((lane & 15) >> 1) == iota((PLANE, COL, 128), 1), wide, 0.0), axis=1)
    for t in range(PLANE):
        rk2s[t] = wide[t : t + 1]
    each(1, PLANE, lambda i: rk2(i).start())
    rk2r[n] = rk2s[n]

    def turn(order, src, dst, q, first, shape):
        for c in range(0, HALF, 256):
            rows = jnp.dot(order[...], src[q, :, :, c : c + 256].reshape(CR, 256), preferred_element_type=F32)
            dst[q, :, :, first + c : first + c + 256] = rows.astype(BF16).reshape(shape)

    def regroup(q):
        got_all(recv1a.at[q, pl.ds(0, COL - 1)], rs1a.at[q])
        stay1a(q).wait()
        turn(by_chip, recv1a, send2a, q, 0, (PLANE, 16, 256))
        each(1, PLANE, lambda i: row2a(q, i).start())
        stay2a(q).start()
        got_all(recv1b.at[q, pl.ds(0, PLANE - 1)], rs1b.at[q])
        stay1b(q).wait()
        turn(by_goal, recv1b, send2b, q, 0, (COL, 32, 256))
        each(1, COL, lambda i: row2b(q, i).start())
        stay2b(q).start()

    def straight(way, q):
        rows = pl.ds(0, STRAIGHT)
        return copy(
            own.at[q, rows], left.at[core, q, rows] if way == 0 else right.at[q, rows],
            ss_ring.at[way], rs_ring.at[way, q], plane_dev(up if way == 0 else down),
        )

    def leg1(d, q):
        _, side, first, last = DETOURS[d]
        return copy(
            own.at[q, pl.ds(first, last - first)], relay.at[d, q, pl.ds(0, last - first)],
            ss_leg1.at[d], rs_leg1.at[d, q], device(n, rem(z + 4 + side, 4), core),
        )

    def leg2(d, q):
        way, side, first, last = DETOURS[d]
        rows = pl.ds(first, last - first)
        return copy(
            relay.at[d, q, pl.ds(0, last - first)], left.at[core, q, rows] if way == 0 else right.at[q, rows],
            ss_leg2.at[d], rs_ring.at[way, q], device(beside[way], rem(z + 4 - side, 4), core),
        )

    def to_sibling(q, k):
        return copy(own.at[q] if k == 0 else left.at[1, q], left.at[k, q], ss_ring.at[2], rs_ring.at[2, q], sibling)

    def rk_ring(way):
        return copy(
            rk_own, rk_left.at[core] if way == 0 else rk_right,
            ss_rank.at[2 + way], rs_rank.at[2 + way], plane_dev(up if way == 0 else down),
        )

    def rk_sibling(k):
        return copy(rk_own if k == 0 else rk_left.at[1], rk_left.at[k], ss_rank.at[4], rs_rank.at[4], sibling)

    def spread_out(q):
        got_all(recv2b.at[q, pl.ds(0, COL - 1)], rs2b.at[q])
        stay2b(q).wait()
        turn(by_chip, recv2b, own, q, HALF, (PLANE, 16, 256))
        got_all(own.at[q, pl.ds(0, PLANE - 1), :, pl.ds(0, HALF)], rs2a.at[q])
        stay2a(q).wait()
        for d in range(len(DETOURS)):
            leg1(d, q).start()
        straight(0, q).start()
        straight(1, q).start()

        @pl.when(core == 0)
        def _():
            to_sibling(q, 0).start()

    def pass_on(q):
        for d in range(len(DETOURS)):
            leg1(d, q).wait_recv()
            leg2(d, q).start()

    regroup(0)

    got_all(rk2r.at[pl.ds(0, PLANE - 1)], rs_rank.at[1])
    got = jnp.concatenate([rk2r[t] for t in range(PLANE)], axis=0)
    got = pick(got, m_home[...], 2)
    got = jnp.sum(jnp.where(of_chip, got, 0.0), axis=0, keepdims=True)
    rk_own[...] = jnp.where(got > 0.0, got, jnp.nan)
    rk_ring(0).start()
    rk_ring(1).start()

    @pl.when(core == 0)
    def _():
        rk_sibling(0).start()

    regroup(1)
    spread_out(0)
    regroup(2)
    spread_out(1)
    pass_on(0)
    spread_out(2)
    pass_on(1)

    def stand(row):
        return jnp.broadcast_to(row, (128, SLOTS)).T.reshape(CH, CR, 128)

    lr_own[...] = stand(rk_own[...])

    def compare(rows, lr, other, rr, accs_left, accs_right):
        scores = lax.dot_general(
            jnp.concatenate(rows, axis=0), other, dims, preferred_element_type=F32
        )
        lefts = [[None, None] for _ in rows]
        for h in range(0, other.shape[0], 128):
            rank_right = rr[:, h : h + 128]
            rights = [None, None]
            for i, lr_i in enumerate(lr):
                part = scores[i * CR : (i + 1) * CR, h : h + 128]
                low = jnp.where(rank_right < lr_i, part, -1.0)
                high = jnp.where(rank_right > lr_i, part, -1.0)
                for el, new in enumerate((low, high)):
                    if accs_left is not None:
                        lefts[i][el] = new if lefts[i][el] is None else jnp.maximum(lefts[i][el], new)
                    new = jnp.max(new.reshape(32, 8, 128), axis=0)
                    rights[1 - el] = new if rights[1 - el] is None else jnp.maximum(rights[1 - el], new)
            for el in range(2):
                accs_right[el][:, h : h + 128] = jnp.maximum(accs_right[el][:, h : h + 128], rights[el])
        if accs_left is not None:
            for acc, new in zip(accs_left, lefts, strict=True):
                for el in range(2):
                    acc[el][...] = jnp.maximum(acc[el][...], new[el])

    compare(
        [own[q].reshape(CR, D) for q in range(CH)], [lr_own[q] for q in range(CH)], own[...].reshape(SLOTS, D), rk_own[...],
        None, [acc_right.at[0, el] for el in range(2)],
    )
    pass_on(2)

    rk_ring(0).wait_recv()

    @pl.when(core == 1)
    def _():
        rk_sibling(1).start()

    rk_ring(1).wait_recv()
    rk_sibling(0).wait_recv()
    for a in range(2):
        lr_left[a] = stand(rk_left[a])

    def compare_left(parts, side, first, last):
        other, rr = (own, rk_own) if side == 0 else (right, rk_right)
        cols = pl.ds(first * CR, (last - first) * CR)
        compare(
            [left[a, q].reshape(CR, D) for a, q in parts], [lr_left[a, q] for a, q in parts],
            other[first:last].reshape((last - first) * CR, D), rr[:, first * CR : last * CR],
            [[acc_left.at[a, el, q] for el in range(2)] for a, q in parts],
            [acc_right.at[side, el, :, cols] for el in range(2)],
        )

    for q in range(CH):
        got_all(left.at[core, q], rs_ring.at[0, q])

        @pl.when(core == 1)
        def _():
            to_sibling(q, 1).start()

        got_all(left.at[1 - core, q], rs_ring.at[2, q])
        now = [(0, q), (1, q)]
        compare_left(now, 0, 0, CH)
        got_all(right.at[q], rs_ring.at[1, q])
        compare_left(now, 1, 0, q + 1)
        if q:
            compare_left([(a, p) for a in range(2) for p in range(q)], 1, q, q + 1)
        if q == 0:
            sent_all(send1a.at[:, pl.ds(0, COL - 1)], ss_row.at[0])
            sent_all(send2a.at[:, pl.ds(0, PLANE - 1)], ss_row.at[1])
            sent_all(send1b.at[:, pl.ds(0, PLANE - 1)], ss_row.at[2])
            sent_all(send2b.at[:, pl.ds(0, COL - 1)], ss_row.at[3])
            sent_all(rk1s.at[pl.ds(0, COL - 1)], ss_rank.at[0])
            sent_all(rk2s.at[pl.ds(0, PLANE - 1)], ss_rank.at[1])
            rk_ring(0).wait_send()
            rk_ring(1).wait_send()
            rk_sibling(0).wait_send()

    def back1(i):
        t = rem(n + i, PLANE)
        return copy(b1s.at[t], b1r.at[s], ss_back.at[0], rs_back.at[0], plane_dev(t))

    def back2(i):
        g = rem(me + i, COL)
        return copy(b2s.at[g], b2r.at[me], ss_back.at[1], rs_back.at[1], col_dev(g))

    def lie(acc):
        return jnp.max(acc.reshape(SLOTS, 128).T, axis=0, keepdims=True)

    def flat(acc):
        return jnp.max(acc, axis=0, keepdims=True)

    found = [[lie(acc_left[a, el]) for el in range(2)] for a in range(2)]
    found += [[flat(acc_right[r, el]) for el in range(2)] for r in range(2)]
    found = [jnp.concatenate([jnp.where(of_chip, m, 0.0) for m in f], axis=1) for f in found]
    found = pick(jnp.concatenate(found, axis=0), m_back[...], 3)
    for t in range(PLANE):
        for k in range(4):
            b1s[t, k : k + 1] = found[k * PLANE + t : k * PLANE + t + 1]
    each(1, PLANE, lambda i: back1(i).start())
    b1r[s] = b1s[n]
    got_all(b1r.at[pl.ds(0, PLANE - 1)], rs_back.at[0])

    def of(k):
        return jnp.concatenate([b1r[t, k : k + 1] for t in range(PLANE)], axis=0)

    def above(m):
        return jnp.concatenate([m[1:], m[:1]], axis=0)

    def below(m):
        return jnp.concatenate([m[PLANE - 1 :], m[: PLANE - 1]], axis=0)

    left0, left1, right0, right1 = of(0), above(of(1)), of(2), below(of(3))
    even = jnp.where(core == 0, jnp.maximum(jnp.maximum(right0, above(left0)), right1), left0)
    uneven = jnp.where(core == 0, left1, jnp.maximum(jnp.maximum(right0, left1), right1))
    wide = jnp.stack([even, uneven])[:, None]
    shape = (2, COL, PLANE, 128)
    wide = jnp.where(((iota(shape, 3) & 15) >> 1) == iota(shape, 1), wide, 0.0)
    wide = pick(wide.reshape(2 * COL * PLANE, 128), unfold[...], 3).reshape(2, COL, PLANE, 256)
    shape = (2, COL, PLANE, 256)
    wide = jnp.sum(jnp.where(((iota(shape, 3) & 31) >> 1) == iota(shape, 2), wide, 0.0), axis=2)
    wide = jnp.concatenate([wide[0], wide[1]], axis=1)
    for g in range(COL):
        b2s[g] = wide[g : g + 1]
    each(1, COL, lambda i: back2(i).start())
    b2r[me] = b2s[me]
    got_all(b2r.at[pl.ds(0, COL - 1)], rs_back.at[1])
    got = jnp.concatenate([b2r[g] for g in range(COL)], axis=0)
    got = jnp.maximum(got[:4], got[4:])
    got = jnp.concatenate([got[:, c : c + 128] for c in (0, 256, 128, 384)], axis=0)
    got = pick(got, at_back, 3)
    out_early[...] = jnp.sum(jnp.where(at_goal, got[:COL], 0.0), axis=0)
    out_late[...] = jnp.sum(jnp.where(at_goal, got[COL:], 0.0), axis=0)

    for way in range(2):
        sent_all(own.at[:, pl.ds(0, STRAIGHT)], ss_ring.at[way])
    sent_all(own, ss_ring.at[2])
    for d, (_, _, first, last) in enumerate(DETOURS):
        sent_all(own.at[:, pl.ds(first, last - first)], ss_leg1.at[d])
        sent_all(relay.at[d, :, pl.ds(0, last - first)], ss_leg2.at[d])
    sent_all(b1s.at[pl.ds(0, PLANE - 1)], ss_back.at[0])
    sent_all(b2s.at[pl.ds(0, COL - 1)], ss_back.at[1])


def body(embeddings, ranks, routes):
    dma = pltpu.SemaphoreType.DMA
    vm = pltpu.VMEM
    here = pl.BlockSpec(memory_space=vm)
    return tuple(pl.pallas_call(
        kernel,
        out_shape=[jax.ShapeDtypeStruct((ROWS,), F32)] * 2,
        in_specs=[pl.BlockSpec(memory_space=pltpu.HBM)] * 3,
        out_specs=[here] * 2,
        scratch_shapes=[
            vm((ROWS, D), F32),
            vm((ROWS,), jnp.int32),
            vm((1, ROWS), jnp.int32),
            vm((CH, COL, 32, HALF), BF16),
            vm((CH, COL, 32, HALF), BF16),
            vm((CH, PLANE, 16, HALF), BF16),
            vm((CH, PLANE, 16, HALF), BF16),
            vm((CH, PLANE, 16, HALF), BF16),
            vm((CH, COL, 32, HALF), BF16),
            vm((CH, COL, 32, HALF), BF16),
            vm((CH, PLANE, 16, D), BF16),
            vm((2, CH, PLANE, 16, D), BF16),
            vm((CH, PLANE, 16, D), BF16),
            vm((4, CH, 3, 16, D), BF16),
            vm((COL, 1, 128), F32),
            vm((COL, 1, 128), F32),
            vm((PLANE, 1, 128), F32),
            vm((PLANE, 1, 128), F32),
            vm((1, SLOTS), F32),
            vm((2, 1, SLOTS), F32),
            vm((1, SLOTS), F32),
            vm((CH, CR, 128), F32),
            vm((2, CH, CR, 128), F32),
            vm((2, 2, CH, CR, 128), F32),
            vm((2, 2, 8, SLOTS), F32),
            vm((PLANE, 4, 128), F32),
            vm((PLANE, 4, 128), F32),
            vm((COL, 1, 512), F32),
            vm((COL, 1, 512), F32),
            vm((CR, CR), BF16),
            vm((CR, CR), BF16),
            vm((128, SLOTS), BF16),
            vm((2 * SLOTS, 128), BF16),
            vm((128, 256), BF16),
            dma((4,)), dma((CH,)), dma((CH,)), dma((CH,)), dma((CH,)),
            dma((5,)), dma((5,)),
            dma((3,)), dma((3, CH)),
            dma((4,)), dma((4, CH)), dma((4,)),
            dma((2,)), dma((2,)),
            dma((4, CH)), dma((3,)),
        ],
        compiler_params=pltpu.CompilerParams(
            collective_id=0, has_side_effects=True, vmem_limit_bytes=VMEM_LIMIT
        ),
    )(embeddings, ranks, routes.reshape(1, ROWS)))


def solution(mesh):
    placed = (P(("group", "blk"), None), P(("group", "blk")), P(("group", "blk"), None))
    return jax.shard_map(
        body,
        mesh=mesh,
        in_specs=placed,
        out_specs=(P(("group", "blk")), P(("group", "blk"))),
        check_vma=False,
    )
```

```python
import jax
import jax.numpy as jnp
from jax import lax
from jax.experimental import pallas as pl
from jax.experimental.pallas import tpu as pltpu
from jax.sharding import PartitionSpec as P

MESH = pl.DeviceIdType.MESH
F32 = jnp.float32
BF16 = jnp.bfloat16

D = 1024
VMEM_LIMIT = 62 * 2**20
HALF = 512
ROWS = 384
SLOTS = 768
CH = 3
CR = 256
COL = 8
PLANE = 16

RINGS = (
    (0, 4, 8, 12, 13, 1, 5, 9, 10, 14, 2, 6, 7, 11, 15, 3),
    (0, 1, 2, 3, 7, 4, 5, 6, 10, 11, 8, 9, 13, 14, 15, 12),
)
PLACES = tuple(tuple(r.index(n) for n in range(PLANE)) for r in RINGS)
UPS = tuple(tuple(r[(r.index(n) + 1) % PLANE] for n in range(PLANE)) for r in RINGS)
DOWNS = tuple(tuple(r[(r.index(n) - 1) % PLANE] for n in range(PLANE)) for r in RINGS)
STRAIGHT = (12, 11, 12)
DETOURS = ((0, 1, 0), (0, -1, 1), (1, -1, 0), (1, 1, 1))


def span(share, q):
    first = STRAIGHT[q]
    middle = first + (PLANE - first + 1) // 2
    return (first, middle) if share == 0 else (middle, PLANE)


def iota(shape, dim):
    return lax.broadcasted_iota(jnp.int32, shape, dim)


def hot(mask):
    return jnp.where(mask, 1.0, 0.0).astype(BF16)


def pick(x, onehot, parts):
    rows = x.shape[0]
    pieces = []
    for _ in range(parts):
        piece = x.astype(BF16)
        pieces.append(piece)
        x = x - piece.astype(F32)
    out = jnp.dot(jnp.concatenate(pieces, axis=0), onehot, preferred_element_type=F32)
    total = out[(parts - 1) * rows :]
    for p in range(parts - 2, -1, -1):
        total = total + out[p * rows : (p + 1) * rows]
    return total


def look(tables, odd, index):
    found = index * 0
    for i in range(PLANE):
        found = jnp.where(index == i, jnp.where(odd == 1, tables[1][i], tables[0][i]), found)
    return found


def rem(a, b):
    return lax.rem(a, b)


def device(n, z, core):
    x, y = lax.div(n, 4), rem(n, 4)
    return (rem(y, 2) * 2 + core, lax.div(y, 2) * 16 + x * 4 + z)


def each(first, last, act):
    def step(i, c):
        act(i)
        return c

    lax.fori_loop(first, last, step, 0)


def kernel(
    emb_hbm, ranks_hbm, routes_hbm, out,
    emb, ranks, routes, send1a, recv1a, send2a, send1b, recv1b, send2b, recv2b, own, left, right, relay,
    rk1s, rk1r, rk2s, rk2r, rk_own, rk_left, rk_right,
    lr_own, lr_left, acc_left, acc_right,
    b1s, b1r, b2s, b2r, by_chip, by_goal, m_home, m_back, unfold,
    ss_row, rs1a, rs2a, rs1b, rs2b, ss_rank, rs_rank,
    ss_ring, rs_ring, ss_leg1, rs_leg1, ss_leg2, ss_back, rs_back, loc, in_sem,
):
    loads = [
        pltpu.make_async_copy(src, dst, in_sem.at[i])
        for i, (src, dst) in enumerate(((routes_hbm, routes), (ranks_hbm, ranks), (emb_hbm, emb)))
    ]
    for load in loads:
        load.start()
    grp = lax.axis_index("group")
    blk = lax.axis_index("blk")
    z, core = rem(blk, 4), rem(grp, 2)
    n = rem(lax.div(blk, 4), 4) * 4 + lax.div(blk, 16) * 2 + lax.div(grp, 2)
    me = core * 4 + z
    odd = rem(z, 2)

    def col_dev(g):
        return device(n, rem(g, 4), lax.div(g, 4))

    def plane_dev(t):
        return device(t, z, core)

    sibling = device(n, z, 1 - core)

    barrier = pltpu.get_barrier_semaphore()

    def greet(to):
        pl.semaphore_signal(barrier, inc=1, device_id=to, device_id_type=MESH)

    each(1, PLANE, lambda i: greet(plane_dev(rem(n + i, PLANE))))
    each(1, COL, lambda i: greet(col_dev(rem(me + i, COL))))
    s = look(PLACES, odd, n)
    up, down = look(UPS, odd, n), look(DOWNS, odd, n)
    beside = (look(UPS, 1 - odd, n), look(DOWNS, 1 - odd, n))
    for way, side, _ in DETOURS:
        greet(device(down if way == 0 else up, rem(z + 4 + side, 4), core))

    loads[0].wait()
    loads[1].wait()
    target = routes[...].reshape(1, ROWS)
    rank = ranks[...].reshape(1, ROWS).astype(F32) + 1.0
    spread = iota((128, ROWS), 0) == target
    before = hot(iota((ROWS, ROWS), 0) < iota((ROWS, ROWS), 1))
    count = jnp.dot(hot(spread), before, preferred_element_type=F32)
    slot = jnp.sum(jnp.where(spread, count, 0.0), axis=0, keepdims=True).astype(jnp.int32)
    cluster, block = target >> 5, target & 31
    goal = (block & 1) * 4 + cluster
    ring = block >> 1
    to_chip = look(RINGS, cluster & 1, ring)
    chunk, two = slot >> 1, slot & 1
    at_goal = iota((COL, ROWS), 0) == goal
    at_spot = hot(iota((128, ROWS), 0) == chunk * 32 + to_chip * 2 + two)
    at_back = hot(iota((128, ROWS), 0) == chunk * 32 + ring * 2 + two)
    ranks16 = jnp.concatenate([jnp.where(at_goal, rank, 0.0), jnp.zeros((COL, ROWS), F32)], axis=0)
    hi = ranks16.astype(BF16)
    lo = (ranks16 - hi.astype(F32)).astype(BF16)
    dims = (((1,), (1,)), ((), ()))
    packed = lax.dot_general(hi, at_spot, dims, preferred_element_type=F32) + lax.dot_general(
        lo, at_spot, dims, preferred_element_type=F32
    )
    for g in range(COL):
        rk1s[g] = packed[g : g + 1]
    loads[2].wait()
    e = emb[...]
    mean_square = jnp.mean(e * e, axis=-1, keepdims=True)
    unit = (e * lax.rsqrt(mean_square + 1e-06) * D ** (-0.5)).astype(BF16)

    def fill(q):
        for index, ref, first, shape in (
            (goal * 32 + to_chip * 2 + two, send1a, 0, (COL, 32, 256)),
            (to_chip * 16 + goal * 2 + two, send1b, HALF, (PLANE, 16, 256)),
        ):
            select = hot(iota((CR, ROWS), 0) == jnp.where(chunk == q, index, -1))
            for c in range(0, HALF, 256):
                rows = jnp.dot(select, unit[:, first + c : first + c + 256], preferred_element_type=F32)
                ref[q, :, :, c : c + 256] = rows.astype(BF16).reshape(shape)

    def copy(src, dst, send, recv, to):
        return pltpu.make_async_remote_copy(
            src_ref=src, dst_ref=dst, send_sem=send, recv_sem=recv, device_id=to, device_id_type=MESH
        )

    def rk1(i):
        g = rem(me + i, COL)
        return copy(rk1s.at[g], rk1r.at[me], ss_rank.at[0], rs_rank.at[0], col_dev(g))

    def rk2(i):
        t = rem(n + i, PLANE)
        return copy(rk2s.at[t], rk2r.at[n], ss_rank.at[1], rs_rank.at[1], plane_dev(t))

    def row1a(q, i):
        g = rem(me + i, COL)
        return copy(send1a.at[q, g], recv1a.at[q, me], ss_row.at[0], rs1a.at[q], col_dev(g))

    def row2a(q, i):
        t = rem(n + i, PLANE)
        return copy(send2a.at[q, t], own.at[q, n, :, pl.ds(0, HALF)], ss_row.at[1], rs2a.at[q], plane_dev(t))

    def row1b(q, i):
        t = rem(n + i, PLANE)
        return copy(send1b.at[q, t], recv1b.at[q, n], ss_row.at[2], rs1b.at[q], plane_dev(t))

    def row2b(q, i):
        g = rem(me + i, COL)
        return copy(send2b.at[q, g], recv2b.at[q, me], ss_row.at[3], rs2b.at[q], col_dev(g))

    def got_all(ref, sem):
        copy(ref, ref, ss_row.at[0], sem, sibling).wait_recv()

    def sent_all(ref, sem):
        copy(ref, ref, sem, rs_rank.at[0], sibling).wait_send()

    def stay1a(q):
        return pltpu.make_async_copy(send1a.at[q, me], recv1a.at[q, me], loc.at[0, q])

    def stay2a(q):
        return pltpu.make_async_copy(send2a.at[q, n], own.at[q, n, :, pl.ds(0, HALF)], loc.at[1, q])

    def stay1b(q):
        return pltpu.make_async_copy(send1b.at[q, n], recv1b.at[q, n], loc.at[2, q])

    def stay2b(q):
        return pltpu.make_async_copy(send2b.at[q, me], recv2b.at[q, me], loc.at[3, q])

    for q in range(CH):
        fill(q)

    a, b = iota((CR, CR), 0), iota((CR, CR), 1)
    by_chip[...] = hot(b == ((a & 15) >> 1) * 32 + (a >> 4) * 2 + (a & 1))
    by_goal[...] = hot(b == ((a & 31) >> 1) * 16 + (a >> 5) * 2 + (a & 1))
    lane = iota((128, SLOTS), 1)
    m_home[...] = hot(iota((128, SLOTS), 0) == (lane >> 8) * 16 + (lane & 15))
    lane = iota((CR, 128), 1)
    same = (lane & 15) == (iota((CR, 128), 0) & 15)
    for i in range(2 * CH):
        m_back[i * CR : (i + 1) * CR] = hot(same & (lane >> 4 == i))
    a, b = iota((128, 256), 0), iota((128, 256), 1)
    unfold[...] = hot(
        (a >> 4 == (b >> 7) * 3 + ((b & 127) >> 5)) & ((a & 1) == (b & 1)) & ((b & 127) < 96)
    )
    acc_left[...] = jnp.full(acc_left.shape, -1.0, F32)
    acc_right[...] = jnp.full(acc_right.shape, -1.0, F32)
    of_chip = ((iota((PLANE, SLOTS), 1) & 255) >> 4) == iota((PLANE, SLOTS), 0)

    pl.semaphore_wait(barrier, COL - 1 + PLANE - 1 + len(DETOURS))
    each(1, COL, lambda i: rk1(i).start())
    for q in range(CH):
        each(1, COL, lambda i: row1a(q, i).start())
        each(1, PLANE, lambda i: row1b(q, i).start())
        stay1a(q).start()
        stay1b(q).start()

    rk1r[me] = rk1s[me]
    got_all(rk1r.at[pl.ds(0, COL - 1)], rs_rank.at[0])
    seen = jnp.concatenate([rk1r[g] for g in range(COL)], axis=0)
    lane = iota((PLANE, COL, 128), 2)
    wide = jnp.where(((lane & 31) >> 1) == iota((PLANE, COL, 128), 0), seen[None], 0.0)
    a, b = iota((128, 128), 0), iota((128, 128), 1)
    fold = hot((a >> 5 == b >> 4) & ((a & 1) == (b & 1)) & (a < 96))
    wide = pick(wide.reshape(128, 128), fold, 2).reshape(PLANE, COL, 128)
    wide = jnp.sum(jnp.where(((lane & 15) >> 1) == iota((PLANE, COL, 128), 1), wide, 0.0), axis=1)
    for t in range(PLANE):
        rk2s[t] = wide[t : t + 1]
    each(1, PLANE, lambda i: rk2(i).start())
    rk2r[n] = rk2s[n]

    def turn(order, src, dst, q, first, shape):
        for c in range(0, HALF, 256):
            rows = jnp.dot(order[...], src[q, :, :, c : c + 256].reshape(CR, 256), preferred_element_type=F32)
            dst[q, :, :, first + c : first + c + 256] = rows.astype(BF16).reshape(shape)

    def regroup(q):
        got_all(recv1b.at[q, pl.ds(0, PLANE - 1)], rs1b.at[q])
        stay1b(q).wait()
        turn(by_goal, recv1b, send2b, q, 0, (COL, 32, 256))
        each(1, COL, lambda i: row2b(q, i).start())
        stay2b(q).start()
        got_all(recv1a.at[q, pl.ds(0, COL - 1)], rs1a.at[q])
        stay1a(q).wait()
        turn(by_chip, recv1a, send2a, q, 0, (PLANE, 16, 256))
        each(1, PLANE, lambda i: row2a(q, i).start())
        stay2a(q).start()

    def straight(way, q):
        rows = pl.ds(0, STRAIGHT[q])
        return copy(
            own.at[q, rows], left.at[core, q, rows] if way == 0 else right.at[q, rows],
            ss_ring.at[way, q], rs_ring.at[way, q], plane_dev(up if way == 0 else down),
        )

    def leg1(d, q):
        _, side, share = DETOURS[d]
        first, last = span(share, q)
        return copy(
            own.at[q, pl.ds(first, last - first)], relay.at[d, q, pl.ds(0, last - first)],
            ss_leg1.at[d, q], rs_leg1.at[d, q], device(n, rem(z + 4 + side, 4), core),
        )

    def leg2(d, q):
        way, side, share = DETOURS[d]
        first, last = span(share, q)
        rows = pl.ds(first, last - first)
        return copy(
            relay.at[d, q, pl.ds(0, last - first)], left.at[core, q, rows] if way == 0 else right.at[q, rows],
            ss_leg2.at[d, q], rs_ring.at[way, q], device(beside[way], rem(z + 4 - side, 4), core),
        )

    def to_sibling(q, k):
        return copy(own.at[q] if k == 0 else left.at[1, q], left.at[k, q], ss_ring.at[2, q], rs_ring.at[2, q], sibling)

    def rk_ring(way):
        return copy(
            rk_own, rk_left.at[core] if way == 0 else rk_right,
            ss_rank.at[2 + way], rs_rank.at[2 + way], plane_dev(up if way == 0 else down),
        )

    def rk_sibling(k):
        return copy(rk_own if k == 0 else rk_left.at[1], rk_left.at[k], ss_rank.at[4], rs_rank.at[4], sibling)

    def spread_out(q):
        got_all(recv2b.at[q, pl.ds(0, COL - 1)], rs2b.at[q])
        stay2b(q).wait()
        turn(by_chip, recv2b, own, q, HALF, (PLANE, 16, 256))
        got_all(own.at[q, pl.ds(0, PLANE - 1), :, pl.ds(0, HALF)], rs2a.at[q])
        stay2a(q).wait()
        for d in range(len(DETOURS)):
            leg1(d, q).start()
        straight(0, q).start()
        straight(1, q).start()

        @pl.when(core == 0)
        def _():
            to_sibling(q, 0).start()

    def pass_on(q):
        for d in range(len(DETOURS)):
            leg1(d, q).wait_recv()
            leg2(d, q).start()

    regroup(0)

    got_all(rk2r.at[pl.ds(0, PLANE - 1)], rs_rank.at[1])
    got = jnp.concatenate([rk2r[t] for t in range(PLANE)], axis=0)
    got = pick(got, m_home[...], 2)
    got = jnp.sum(jnp.where(of_chip, got, 0.0), axis=0, keepdims=True)
    rk_own[...] = jnp.where(got > 0.0, got, jnp.nan)
    rk_ring(0).start()
    rk_ring(1).start()

    @pl.when(core == 0)
    def _():
        rk_sibling(0).start()

    regroup(1)
    spread_out(0)
    regroup(2)
    spread_out(1)
    pass_on(0)
    spread_out(2)
    pass_on(1)

    def stand(row):
        return jnp.broadcast_to(row, (128, SLOTS)).T.reshape(CH, CR, 128)

    lr_own[...] = stand(rk_own[...])

    def compare(rows, lr, other, rr, accs_left, accs_right):
        scores = lax.dot_general(
            jnp.concatenate(rows, axis=0), other, dims, preferred_element_type=F32
        )
        lefts = [[None, None] for _ in rows]
        for h in range(0, other.shape[0], 128):
            rank_right = rr[:, h : h + 128]
            rights = [None, None]
            for i, lr_i in enumerate(lr):
                part = scores[i * CR : (i + 1) * CR, h : h + 128]
                low = jnp.where(rank_right < lr_i, part, -1.0)
                high = jnp.where(rank_right > lr_i, part, -1.0)
                for el, new in enumerate((low, high)):
                    if accs_left is not None:
                        lefts[i][el] = new if lefts[i][el] is None else jnp.maximum(lefts[i][el], new)
                    new = jnp.max(new.reshape(32, 8, 128), axis=0)
                    rights[1 - el] = new if rights[1 - el] is None else jnp.maximum(rights[1 - el], new)
            for el in range(2):
                accs_right[el][:, h : h + 128] = jnp.maximum(accs_right[el][:, h : h + 128], rights[el])
        if accs_left is not None:
            for acc, new in zip(accs_left, lefts, strict=True):
                for el in range(2):
                    acc[el][...] = jnp.maximum(acc[el][...], new[el])

    compare(
        [own[q].reshape(CR, D) for q in range(CH)], [lr_own[q] for q in range(CH)], own[...].reshape(SLOTS, D), rk_own[...],
        None, [acc_right.at[0, el] for el in range(2)],
    )
    pass_on(2)

    rk_ring(0).wait_recv()

    @pl.when(core == 1)
    def _():
        rk_sibling(1).start()

    rk_ring(1).wait_recv()
    rk_sibling(0).wait_recv()
    for a in range(2):
        lr_left[a] = stand(rk_left[a])

    def compare_left(parts, side, first, last):
        other, rr = (own, rk_own) if side == 0 else (right, rk_right)
        cols = pl.ds(first * CR, (last - first) * CR)
        compare(
            [left[a, q].reshape(CR, D) for a, q in parts], [lr_left[a, q] for a, q in parts],
            other[first:last].reshape((last - first) * CR, D), rr[:, first * CR : last * CR],
            [[acc_left.at[a, el, q] for el in range(2)] for a, q in parts],
            [acc_right.at[side, el, :, cols] for el in range(2)],
        )

    for q in range(CH):
        got_all(left.at[core, q], rs_ring.at[0, q])

        @pl.when(core == 1)
        def _():
            to_sibling(q, 1).start()

        got_all(left.at[1 - core, q], rs_ring.at[2, q])
        now = [(0, q), (1, q)]
        compare_left(now, 0, 0, CH)
        got_all(right.at[q], rs_ring.at[1, q])
        compare_left(now, 1, 0, q + 1)
        if q:
            compare_left([(a, p) for a in range(2) for p in range(q)], 1, q, q + 1)
        if q == 0:
            sent_all(send1a.at[:, pl.ds(0, COL - 1)], ss_row.at[0])
            sent_all(send2a.at[:, pl.ds(0, PLANE - 1)], ss_row.at[1])
            sent_all(send1b.at[:, pl.ds(0, PLANE - 1)], ss_row.at[2])
            sent_all(send2b.at[:, pl.ds(0, COL - 1)], ss_row.at[3])
            sent_all(rk1s.at[pl.ds(0, COL - 1)], ss_rank.at[0])
            sent_all(rk2s.at[pl.ds(0, PLANE - 1)], ss_rank.at[1])
            rk_ring(0).wait_send()
            rk_ring(1).wait_send()
            rk_sibling(0).wait_send()

    def back1(i):
        t = rem(n + i, PLANE)
        return copy(b1s.at[t], b1r.at[s], ss_back.at[0], rs_back.at[0], plane_dev(t))

    def back2(i):
        g = rem(me + i, COL)
        return copy(b2s.at[g], b2r.at[me], ss_back.at[1], rs_back.at[1], col_dev(g))

    def lie(acc):
        return jnp.max(acc.reshape(SLOTS, 128).T, axis=0, keepdims=True)

    def flat(acc):
        return jnp.max(acc, axis=0, keepdims=True)

    found = [[lie(acc_left[a, el]) for el in range(2)] for a in range(2)]
    found += [[flat(acc_right[r, el]) for el in range(2)] for r in range(2)]
    found = [jnp.concatenate([jnp.where(of_chip, m, 0.0) for m in f], axis=1) for f in found]
    found = pick(jnp.concatenate(found, axis=0), m_back[...], 3)
    for t in range(PLANE):
        for k in range(4):
            b1s[t, k : k + 1] = found[k * PLANE + t : k * PLANE + t + 1]
    each(1, PLANE, lambda i: back1(i).start())
    b1r[s] = b1s[n]
    got_all(b1r.at[pl.ds(0, PLANE - 1)], rs_back.at[0])

    def of(k):
        return jnp.concatenate([b1r[t, k : k + 1] for t in range(PLANE)], axis=0)

    def above(m):
        return jnp.concatenate([m[1:], m[:1]], axis=0)

    def below(m):
        return jnp.concatenate([m[PLANE - 1 :], m[: PLANE - 1]], axis=0)

    left0, left1, right0, right1 = of(0), above(of(1)), of(2), below(of(3))
    even = jnp.where(core == 0, jnp.maximum(jnp.maximum(right0, above(left0)), right1), left0)
    uneven = jnp.where(core == 0, left1, jnp.maximum(jnp.maximum(right0, left1), right1))
    wide = jnp.stack([even, uneven])[:, None]
    shape = (2, COL, PLANE, 128)
    wide = jnp.where(((iota(shape, 3) & 15) >> 1) == iota(shape, 1), wide, 0.0)
    wide = pick(wide.reshape(2 * COL * PLANE, 128), unfold[...], 3).reshape(2, COL, PLANE, 256)
    shape = (2, COL, PLANE, 256)
    wide = jnp.sum(jnp.where(((iota(shape, 3) & 31) >> 1) == iota(shape, 2), wide, 0.0), axis=2)
    wide = jnp.concatenate([wide[0], wide[1]], axis=1)
    for g in range(COL):
        b2s[g] = wide[g : g + 1]
    each(1, COL, lambda i: back2(i).start())
    b2r[me] = b2s[me]
    got_all(b2r.at[pl.ds(0, COL - 1)], rs_back.at[1])
    got = jnp.concatenate([b2r[g] for g in range(COL)], axis=0)
    got = jnp.maximum(got[:4], got[4:])
    got = jnp.concatenate([got[:, c : c + 128] for c in (0, 256, 128, 384)], axis=0)
    got = pick(got, at_back, 3)
    out[0:1] = jnp.sum(jnp.where(at_goal, got[:COL], 0.0), axis=0, keepdims=True)
    out[1:2] = jnp.sum(jnp.where(at_goal, got[COL:], 0.0), axis=0, keepdims=True)

    for q in range(CH):
        for way in range(2):
            sent_all(own.at[q, pl.ds(0, STRAIGHT[q])], ss_ring.at[way, q])
        sent_all(own.at[q], ss_ring.at[2, q])
        for d, (_, _, share) in enumerate(DETOURS):
            first, last = span(share, q)
            sent_all(own.at[q, pl.ds(first, last - first)], ss_leg1.at[d, q])
            sent_all(relay.at[d, q, pl.ds(0, last - first)], ss_leg2.at[d, q])
    sent_all(b1s.at[pl.ds(0, PLANE - 1)], ss_back.at[0])
    sent_all(b2s.at[pl.ds(0, COL - 1)], ss_back.at[1])


def body(embeddings, ranks, routes):
    dma = pltpu.SemaphoreType.DMA
    vm = pltpu.VMEM
    here = pl.BlockSpec(memory_space=vm)
    out = pl.pallas_call(
        kernel,
        out_shape=jax.ShapeDtypeStruct((2, ROWS), F32),
        in_specs=[pl.BlockSpec(memory_space=pltpu.HBM)] * 3,
        out_specs=here,
        scratch_shapes=[
            vm((ROWS, D), F32),
            vm((ROWS,), jnp.int32),
            vm((1, ROWS), jnp.int32),
            vm((CH, COL, 32, HALF), BF16),
            vm((CH, COL, 32, HALF), BF16),
            vm((CH, PLANE, 16, HALF), BF16),
            vm((CH, PLANE, 16, HALF), BF16),
            vm((CH, PLANE, 16, HALF), BF16),
            vm((CH, COL, 32, HALF), BF16),
            vm((CH, COL, 32, HALF), BF16),
            vm((CH, PLANE, 16, D), BF16),
            vm((2, CH, PLANE, 16, D), BF16),
            vm((CH, PLANE, 16, D), BF16),
            vm((4, CH, 4, 16, D), BF16),
            vm((COL, 1, 128), F32),
            vm((COL, 1, 128), F32),
            vm((PLANE, 1, 128), F32),
            vm((PLANE, 1, 128), F32),
            vm((1, SLOTS), F32),
            vm((2, 1, SLOTS), F32),
            vm((1, SLOTS), F32),
            vm((CH, CR, 128), F32),
            vm((2, CH, CR, 128), F32),
            vm((2, 2, CH, CR, 128), F32),
            vm((2, 2, 8, SLOTS), F32),
            vm((PLANE, 4, 128), F32),
            vm((PLANE, 4, 128), F32),
            vm((COL, 1, 512), F32),
            vm((COL, 1, 512), F32),
            vm((CR, CR), BF16),
            vm((CR, CR), BF16),
            vm((128, SLOTS), BF16),
            vm((2 * SLOTS, 128), BF16),
            vm((128, 256), BF16),
            dma((4,)), dma((CH,)), dma((CH,)), dma((CH,)), dma((CH,)),
            dma((5,)), dma((5,)),
            dma((3, CH)), dma((3, CH)),
            dma((4, CH)), dma((4, CH)), dma((4, CH)),
            dma((2,)), dma((2,)),
            dma((4, CH)), dma((3,)),
        ],
        compiler_params=pltpu.CompilerParams(
            collective_id=0, has_side_effects=True, vmem_limit_bytes=VMEM_LIMIT
        ),
    )(embeddings, ranks, routes.reshape(1, ROWS))
    return out[0], out[1]


def solution(mesh):
    placed = (P(("group", "blk"), None), P(("group", "blk")), P(("group", "blk"), None))
    return jax.shard_map(
        body,
        mesh=mesh,
        in_specs=placed,
        out_specs=(P(("group", "blk")), P(("group", "blk"))),
        check_vma=False,
    )
```

```python
import jax
import jax.numpy as jnp
from jax import lax
from jax.experimental import pallas as pl
from jax.experimental.pallas import tpu as pltpu
from jax.sharding import PartitionSpec as P

MESH = pl.DeviceIdType.MESH
F32 = jnp.float32
BF16 = jnp.bfloat16

D = 1024
VMEM_LIMIT = 62 * 2**20
HALF = 512
ROWS = 384
SLOTS = 768
CH = 3
CR = 256
COL = 8
PLANE = 16

RINGS = (
    (0, 4, 8, 12, 13, 1, 5, 9, 10, 14, 2, 6, 7, 11, 15, 3),
    (0, 1, 2, 3, 7, 4, 5, 6, 10, 11, 8, 9, 13, 14, 15, 12),
)
PLACES = tuple(tuple(r.index(n) for n in range(PLANE)) for r in RINGS)
UPS = tuple(tuple(r[(r.index(n) + 1) % PLANE] for n in range(PLANE)) for r in RINGS)
DOWNS = tuple(tuple(r[(r.index(n) - 1) % PLANE] for n in range(PLANE)) for r in RINGS)
STRAIGHT = (11, 12, 11)
DETOURS = ((0, 1, 0), (0, -1, 1), (1, -1, 0), (1, 1, 1))


def span(share, q):
    first = STRAIGHT[q]
    middle = first + (PLANE - first + 1) // 2
    return (first, middle) if share == 0 else (middle, PLANE)


MIXED = (10, 1, 4, 3, 12, 2, 8, 5, 15, 7, 13, 6, 9, 14, 11)


def iota(shape, dim):
    return lax.broadcasted_iota(jnp.int32, shape, dim)


def hot(mask):
    return jnp.where(mask, 1.0, 0.0).astype(BF16)


def pick(x, onehot, parts):
    rows = x.shape[0]
    pieces = []
    for _ in range(parts):
        piece = x.astype(BF16)
        pieces.append(piece)
        x = x - piece.astype(F32)
    out = jnp.dot(jnp.concatenate(pieces, axis=0), onehot, preferred_element_type=F32)
    total = out[(parts - 1) * rows :]
    for p in range(parts - 2, -1, -1):
        total = total + out[p * rows : (p + 1) * rows]
    return total


def look(tables, odd, index):
    found = index * 0
    for i in range(PLANE):
        found = jnp.where(index == i, jnp.where(odd == 1, tables[1][i], tables[0][i]), found)
    return found


def rem(a, b):
    return lax.rem(a, b)


def device(n, z, core):
    x, y = lax.div(n, 4), rem(n, 4)
    return (rem(y, 2) * 2 + core, lax.div(y, 2) * 16 + x * 4 + z)


def each(first, last, act):
    for i in range(first, last):
        act(i)


def kernel(
    emb_hbm, ranks_hbm, routes_hbm, out,
    emb, ranks, routes, send1a, recv1a, send2a, send1b, recv1b, send2b, recv2b, own, left, right, relay,
    rk1s, rk1r, rk2s, rk2r, rk_own, rk_left, rk_right,
    lr_own, lr_left, acc_left, acc_right,
    b1s, b1r, b2s, b2r, by_chip, by_goal, m_home, m_back, unfold,
    ss_row, rs1a, rs2a, rs1b, rs2b, ss_rank, rs_rank,
    ss_ring, rs_ring, ss_leg1, rs_leg1, ss_leg2, ss_back, rs_back, loc, in_sem,
):
    loads = [
        pltpu.make_async_copy(src, dst, in_sem.at[i])
        for i, (src, dst) in enumerate(((routes_hbm, routes), (ranks_hbm, ranks), (emb_hbm, emb)))
    ]
    for load in loads:
        load.start()
    grp = lax.axis_index("group")
    blk = lax.axis_index("blk")
    z, core = rem(blk, 4), rem(grp, 2)
    n = rem(lax.div(blk, 4), 4) * 4 + lax.div(blk, 16) * 2 + lax.div(grp, 2)
    me = core * 4 + z
    odd = rem(z, 2)

    def col_dev(g):
        return device(n, rem(g, 4), lax.div(g, 4))

    def plane_dev(t):
        return device(t, z, core)

    sibling = device(n, z, 1 - core)

    barrier = pltpu.get_barrier_semaphore()

    def greet(to):
        pl.semaphore_signal(barrier, inc=1, device_id=to, device_id_type=MESH)

    for i in MIXED:
        greet(plane_dev(rem(n + i, PLANE)))
    each(1, COL, lambda i: greet(col_dev(rem(me + i, COL))))

    loads[0].wait()
    loads[1].wait()
    target = routes[...].reshape(1, ROWS)
    rank = ranks[...].reshape(1, ROWS).astype(F32) + 1.0
    spread = iota((128, ROWS), 0) == target
    before = hot(iota((ROWS, ROWS), 0) < iota((ROWS, ROWS), 1))
    count = jnp.dot(hot(spread), before, preferred_element_type=F32)
    slot = jnp.sum(jnp.where(spread, count, 0.0), axis=0, keepdims=True).astype(jnp.int32)
    cluster, block = target >> 5, target & 31
    goal = (block & 1) * 4 + cluster
    ring = block >> 1
    to_chip = look(RINGS, cluster & 1, ring)
    chunk, two = slot >> 1, slot & 1
    at_goal = iota((COL, ROWS), 0) == goal
    at_spot = hot(iota((128, ROWS), 0) == chunk * 32 + to_chip * 2 + two)
    at_back = hot(iota((128, ROWS), 0) == chunk * 32 + ring * 2 + two)
    ranks16 = jnp.concatenate([jnp.where(at_goal, rank, 0.0), jnp.zeros((COL, ROWS), F32)], axis=0)
    hi = ranks16.astype(BF16)
    lo = (ranks16 - hi.astype(F32)).astype(BF16)
    dims = (((1,), (1,)), ((), ()))
    packed = lax.dot_general(hi, at_spot, dims, preferred_element_type=F32) + lax.dot_general(
        lo, at_spot, dims, preferred_element_type=F32
    )
    for g in range(COL):
        rk1s[g] = packed[g : g + 1]
    loads[2].wait()
    e = emb[...]
    mean_square = jnp.mean(e * e, axis=-1, keepdims=True)
    unit = (e * lax.rsqrt(mean_square + 1e-06) * D ** (-0.5)).astype(BF16)

    def fill(q):
        for index, ref, first, shape in (
            (goal * 32 + to_chip * 2 + two, send1a, 0, (COL, 32, 256)),
            (to_chip * 16 + goal * 2 + two, send1b, HALF, (PLANE, 16, 256)),
        ):
            select = hot(iota((CR, ROWS), 0) == jnp.where(chunk == q, index, -1))
            for c in range(0, HALF, 256):
                rows = jnp.dot(select, unit[:, first + c : first + c + 256], preferred_element_type=F32)
                ref[q, :, :, c : c + 256] = rows.astype(BF16).reshape(shape)

    def copy(src, dst, send, recv, to):
        return pltpu.make_async_remote_copy(
            src_ref=src, dst_ref=dst, send_sem=send, recv_sem=recv, device_id=to, device_id_type=MESH
        )

    def rk1(i):
        g = rem(me + i, COL)
        return copy(rk1s.at[g], rk1r.at[me], ss_rank.at[0], rs_rank.at[0], col_dev(g))

    def rk2(i):
        t = rem(n + i, PLANE)
        return copy(rk2s.at[t], rk2r.at[n], ss_rank.at[1], rs_rank.at[1], plane_dev(t))

    def row1a(q, i):
        g = rem(me + i, COL)
        return copy(send1a.at[q, g], recv1a.at[q, me], ss_row.at[0], rs1a.at[q], col_dev(g))

    def row2a(q, i):
        t = rem(n + i, PLANE)
        return copy(send2a.at[q, t], own.at[q, n, :, pl.ds(0, HALF)], ss_row.at[1], rs2a.at[q], plane_dev(t))

    def row1b(q, i):
        t = rem(n + i, PLANE)
        return copy(send1b.at[q, t], recv1b.at[q, n], ss_row.at[2], rs1b.at[q], plane_dev(t))

    def row2b(q, i):
        g = rem(me + i, COL)
        return copy(send2b.at[q, g], recv2b.at[q, me], ss_row.at[3], rs2b.at[q], col_dev(g))

    def got_all(ref, sem):
        copy(ref, ref, ss_row.at[0], sem, sibling).wait_recv()

    def sent_all(ref, sem):
        copy(ref, ref, sem, rs_rank.at[0], sibling).wait_send()

    def stay1a(q):
        return pltpu.make_async_copy(send1a.at[q, me], recv1a.at[q, me], loc.at[0, q])

    def stay2a(q):
        return pltpu.make_async_copy(send2a.at[q, n], own.at[q, n, :, pl.ds(0, HALF)], loc.at[1, q])

    def stay1b(q):
        return pltpu.make_async_copy(send1b.at[q, n], recv1b.at[q, n], loc.at[2, q])

    def stay2b(q):
        return pltpu.make_async_copy(send2b.at[q, me], recv2b.at[q, me], loc.at[3, q])

    for q in range(CH):
        fill(q)

    s = look(PLACES, odd, n)
    up, down = look(UPS, odd, n), look(DOWNS, odd, n)
    beside = (look(UPS, 1 - odd, n), look(DOWNS, 1 - odd, n))

    a, b = iota((CR, CR), 0), iota((CR, CR), 1)
    by_chip[...] = hot(b == ((a & 15) >> 1) * 32 + (a >> 4) * 2 + (a & 1))
    by_goal[...] = hot(b == ((a & 31) >> 1) * 16 + (a >> 5) * 2 + (a & 1))
    lane = iota((128, SLOTS), 1)
    m_home[...] = hot(iota((128, SLOTS), 0) == (lane >> 8) * 16 + (lane & 15))
    lane = iota((CR, 128), 1)
    same = (lane & 15) == (iota((CR, 128), 0) & 15)
    for i in range(2 * CH):
        m_back[i * CR : (i + 1) * CR] = hot(same & (lane >> 4 == i))
    a, b = iota((128, 256), 0), iota((128, 256), 1)
    unfold[...] = hot(
        (a >> 4 == (b >> 7) * 3 + ((b & 127) >> 5)) & ((a & 1) == (b & 1)) & ((b & 127) < 96)
    )
    acc_left[...] = jnp.full(acc_left.shape, -1.0, F32)
    acc_right[...] = jnp.full(acc_right.shape, -1.0, F32)
    of_chip = ((iota((PLANE, SLOTS), 1) & 255) >> 4) == iota((PLANE, SLOTS), 0)

    pl.semaphore_wait(barrier, COL - 1 + PLANE - 1)
    each(1, COL, lambda i: rk1(i).start())
    for q in range(CH):
        for i, t in enumerate(MIXED):
            row1b(q, t).start()
            if i % 2 == 0 and i // 2 + 1 < COL:
                row1a(q, i // 2 + 1).start()
        stay1a(q).start()
        stay1b(q).start()

    rk1r[me] = rk1s[me]
    got_all(rk1r.at[pl.ds(0, COL - 1)], rs_rank.at[0])
    seen = jnp.concatenate([rk1r[g] for g in range(COL)], axis=0)
    lane = iota((PLANE, COL, 128), 2)
    wide = jnp.where(((lane & 31) >> 1) == iota((PLANE, COL, 128), 0), seen[None], 0.0)
    a, b = iota((128, 128), 0), iota((128, 128), 1)
    fold = hot((a >> 5 == b >> 4) & ((a & 1) == (b & 1)) & (a < 96))
    wide = pick(wide.reshape(128, 128), fold, 2).reshape(PLANE, COL, 128)
    wide = jnp.sum(jnp.where(((lane & 15) >> 1) == iota((PLANE, COL, 128), 1), wide, 0.0), axis=1)
    for t in range(PLANE):
        rk2s[t] = wide[t : t + 1]
    each(1, PLANE, lambda i: rk2(i).start())
    rk2r[n] = rk2s[n]

    def turn(order, src, dst, q, first, shape):
        for c in range(0, HALF, 256):
            rows = jnp.dot(order[...], src[q, :, :, c : c + 256].reshape(CR, 256), preferred_element_type=F32)
            dst[q, :, :, first + c : first + c + 256] = rows.astype(BF16).reshape(shape)

    def regroup(q):
        got_all(recv1b.at[q, pl.ds(0, PLANE - 1)], rs1b.at[q])
        stay1b(q).wait()
        turn(by_goal, recv1b, send2b, q, 0, (COL, 32, 256))
        each(1, COL, lambda i: row2b(q, i).start())
        stay2b(q).start()
        got_all(recv1a.at[q, pl.ds(0, COL - 1)], rs1a.at[q])
        stay1a(q).wait()
        turn(by_chip, recv1a, send2a, q, 0, (PLANE, 16, 256))
        for i in MIXED:
            row2a(q, i).start()
        stay2a(q).start()

    def straight(way, q):
        rows = pl.ds(0, STRAIGHT[q])
        return copy(
            own.at[q, rows], left.at[core, q, rows] if way == 0 else right.at[q, rows],
            ss_ring.at[way, q], rs_ring.at[way, q], plane_dev(up if way == 0 else down),
        )

    def leg1(d, q):
        _, side, share = DETOURS[d]
        first, last = span(share, q)
        return copy(
            own.at[q, pl.ds(first, last - first)], relay.at[d, q, pl.ds(0, last - first)],
            ss_leg1.at[d, q], rs_leg1.at[d, q], device(n, rem(z + 4 + side, 4), core),
        )

    def leg2(d, q):
        way, side, share = DETOURS[d]
        first, last = span(share, q)
        rows = pl.ds(first, last - first)
        return copy(
            relay.at[d, q, pl.ds(0, last - first)], left.at[core, q, rows] if way == 0 else right.at[q, rows],
            ss_leg2.at[d, q], rs_ring.at[way, q], device(beside[way], rem(z + 4 - side, 4), core),
        )

    def to_sibling(q, k):
        return copy(own.at[q] if k == 0 else left.at[1, q], left.at[k, q], ss_ring.at[2, q], rs_ring.at[2, q], sibling)

    def rk_ring(way):
        return copy(
            rk_own, rk_left.at[core] if way == 0 else rk_right,
            ss_rank.at[2 + way], rs_rank.at[2 + way], plane_dev(up if way == 0 else down),
        )

    def rk_sibling(k):
        return copy(rk_own if k == 0 else rk_left.at[1], rk_left.at[k], ss_rank.at[4], rs_rank.at[4], sibling)

    def spread_out(q):
        got_all(recv2b.at[q, pl.ds(0, COL - 1)], rs2b.at[q])
        stay2b(q).wait()
        turn(by_chip, recv2b, own, q, HALF, (PLANE, 16, 256))
        got_all(own.at[q, pl.ds(0, PLANE - 1), :, pl.ds(0, HALF)], rs2a.at[q])
        stay2a(q).wait()
        for d in range(len(DETOURS)):
            leg1(d, q).start()
        straight(0, q).start()
        straight(1, q).start()

        @pl.when(core == 0)
        def _():
            to_sibling(q, 0).start()

    def pass_on(q):
        for d in range(len(DETOURS)):
            leg1(d, q).wait_recv()
            leg2(d, q).start()

    regroup(0)

    got_all(rk2r.at[pl.ds(0, PLANE - 1)], rs_rank.at[1])
    got = jnp.concatenate([rk2r[t] for t in range(PLANE)], axis=0)
    got = pick(got, m_home[...], 2)
    got = jnp.sum(jnp.where(of_chip, got, 0.0), axis=0, keepdims=True)
    rk_own[...] = jnp.where(got > 0.0, got, jnp.nan)
    rk_ring(0).start()
    rk_ring(1).start()

    @pl.when(core == 0)
    def _():
        rk_sibling(0).start()

    regroup(1)
    spread_out(0)
    regroup(2)
    spread_out(1)
    pass_on(0)
    spread_out(2)
    pass_on(1)

    def stand(row):
        return jnp.broadcast_to(row, (128, SLOTS)).T.reshape(CH, CR, 128)

    lr_own[...] = stand(rk_own[...])

    def compare(rows, lr, other, rr, accs_left, accs_right):
        scores = lax.dot_general(
            jnp.concatenate(rows, axis=0), other, dims, preferred_element_type=F32
        )
        lefts = [[None, None] for _ in rows]
        for h in range(0, other.shape[0], 128):
            rank_right = rr[:, h : h + 128]
            rights = [None, None]
            for i, lr_i in enumerate(lr):
                part = scores[i * CR : (i + 1) * CR, h : h + 128]
                low = jnp.where(rank_right < lr_i, part, -1.0)
                high = jnp.where(rank_right > lr_i, part, -1.0)
                for el, new in enumerate((low, high)):
                    if accs_left is not None:
                        lefts[i][el] = new if lefts[i][el] is None else jnp.maximum(lefts[i][el], new)
                    new = jnp.max(new.reshape(32, 8, 128), axis=0)
                    rights[1 - el] = new if rights[1 - el] is None else jnp.maximum(rights[1 - el], new)
            for el in range(2):
                accs_right[el][:, h : h + 128] = jnp.maximum(accs_right[el][:, h : h + 128], rights[el])
        if accs_left is not None:
            for acc, new in zip(accs_left, lefts, strict=True):
                for el in range(2):
                    acc[el][...] = jnp.maximum(acc[el][...], new[el])

    compare(
        [own[q].reshape(CR, D) for q in range(CH)], [lr_own[q] for q in range(CH)], own[...].reshape(SLOTS, D), rk_own[...],
        None, [acc_right.at[0, el] for el in range(2)],
    )
    pass_on(2)

    rk_ring(0).wait_recv()

    @pl.when(core == 1)
    def _():
        rk_sibling(1).start()

    rk_ring(1).wait_recv()
    rk_sibling(0).wait_recv()
    for a in range(2):
        lr_left[a] = stand(rk_left[a])

    def compare_left(parts, side, first, last):
        other, rr = (own, rk_own) if side == 0 else (right, rk_right)
        cols = pl.ds(first * CR, (last - first) * CR)
        compare(
            [left[a, q].reshape(CR, D) for a, q in parts], [lr_left[a, q] for a, q in parts],
            other[first:last].reshape((last - first) * CR, D), rr[:, first * CR : last * CR],
            [[acc_left.at[a, el, q] for el in range(2)] for a, q in parts],
            [acc_right.at[side, el, :, cols] for el in range(2)],
        )

    for q in range(CH):
        got_all(left.at[core, q], rs_ring.at[0, q])

        @pl.when(core == 1)
        def _():
            to_sibling(q, 1).start()

        got_all(left.at[1 - core, q], rs_ring.at[2, q])
        now = [(0, q), (1, q)]
        compare_left(now, 0, 0, CH)
        got_all(right.at[q], rs_ring.at[1, q])
        compare_left(now, 1, 0, q + 1)
        if q:
            compare_left([(a, p) for a in range(2) for p in range(q)], 1, q, q + 1)
        if q == 0:
            sent_all(send1a.at[:, pl.ds(0, COL - 1)], ss_row.at[0])
            sent_all(send2a.at[:, pl.ds(0, PLANE - 1)], ss_row.at[1])
            sent_all(send1b.at[:, pl.ds(0, PLANE - 1)], ss_row.at[2])
            sent_all(send2b.at[:, pl.ds(0, COL - 1)], ss_row.at[3])
            sent_all(rk1s.at[pl.ds(0, COL - 1)], ss_rank.at[0])
            sent_all(rk2s.at[pl.ds(0, PLANE - 1)], ss_rank.at[1])
            rk_ring(0).wait_send()
            rk_ring(1).wait_send()
            rk_sibling(0).wait_send()

    def back1(i):
        t = rem(n + i, PLANE)
        return copy(b1s.at[t], b1r.at[s], ss_back.at[0], rs_back.at[0], plane_dev(t))

    def back2(i):
        g = rem(me + i, COL)
        return copy(b2s.at[g], b2r.at[me], ss_back.at[1], rs_back.at[1], col_dev(g))

    def lie(acc):
        return jnp.max(acc.reshape(SLOTS, 128).T, axis=0, keepdims=True)

    def flat(acc):
        return jnp.max(acc, axis=0, keepdims=True)

    found = [[lie(acc_left[a, el]) for el in range(2)] for a in range(2)]
    found += [[flat(acc_right[r, el]) for el in range(2)] for r in range(2)]
    found = [jnp.concatenate([jnp.where(of_chip, m, 0.0) for m in f], axis=1) for f in found]
    found = pick(jnp.concatenate(found, axis=0), m_back[...], 3)
    for t in range(PLANE):
        for k in range(4):
            b1s[t, k : k + 1] = found[k * PLANE + t : k * PLANE + t + 1]
    each(1, PLANE, lambda i: back1(i).start())
    b1r[s] = b1s[n]
    got_all(b1r.at[pl.ds(0, PLANE - 1)], rs_back.at[0])

    def of(k):
        return jnp.concatenate([b1r[t, k : k + 1] for t in range(PLANE)], axis=0)

    def above(m):
        return jnp.concatenate([m[1:], m[:1]], axis=0)

    def below(m):
        return jnp.concatenate([m[PLANE - 1 :], m[: PLANE - 1]], axis=0)

    left0, left1, right0, right1 = of(0), above(of(1)), of(2), below(of(3))
    even = jnp.where(core == 0, jnp.maximum(jnp.maximum(right0, above(left0)), right1), left0)
    uneven = jnp.where(core == 0, left1, jnp.maximum(jnp.maximum(right0, left1), right1))
    wide = jnp.stack([even, uneven])[:, None]
    shape = (2, COL, PLANE, 128)
    wide = jnp.where(((iota(shape, 3) & 15) >> 1) == iota(shape, 1), wide, 0.0)
    wide = pick(wide.reshape(2 * COL * PLANE, 128), unfold[...], 3).reshape(2, COL, PLANE, 256)
    shape = (2, COL, PLANE, 256)
    wide = jnp.sum(jnp.where(((iota(shape, 3) & 31) >> 1) == iota(shape, 2), wide, 0.0), axis=2)
    wide = jnp.concatenate([wide[0], wide[1]], axis=1)
    for g in range(COL):
        b2s[g] = wide[g : g + 1]
    each(1, COL, lambda i: back2(i).start())
    b2r[me] = b2s[me]
    got_all(b2r.at[pl.ds(0, COL - 1)], rs_back.at[1])
    got = jnp.concatenate([b2r[g] for g in range(COL)], axis=0)
    got = jnp.maximum(got[:4], got[4:])
    got = jnp.concatenate([got[:, c : c + 128] for c in (0, 256, 128, 384)], axis=0)
    got = pick(got, at_back, 3)
    out[0:1] = jnp.sum(jnp.where(at_goal, got[:COL], 0.0), axis=0, keepdims=True)
    out[1:2] = jnp.sum(jnp.where(at_goal, got[COL:], 0.0), axis=0, keepdims=True)

    for q in range(CH):
        for way in range(2):
            sent_all(own.at[q, pl.ds(0, STRAIGHT[q])], ss_ring.at[way, q])
        sent_all(own.at[q], ss_ring.at[2, q])
        for d, (_, _, share) in enumerate(DETOURS):
            first, last = span(share, q)
            sent_all(own.at[q, pl.ds(first, last - first)], ss_leg1.at[d, q])
            sent_all(relay.at[d, q, pl.ds(0, last - first)], ss_leg2.at[d, q])
    sent_all(b1s.at[pl.ds(0, PLANE - 1)], ss_back.at[0])
    sent_all(b2s.at[pl.ds(0, COL - 1)], ss_back.at[1])


def body(embeddings, ranks, routes):
    dma = pltpu.SemaphoreType.DMA
    vm = pltpu.VMEM
    here = pl.BlockSpec(memory_space=vm)
    out = pl.pallas_call(
        kernel,
        out_shape=jax.ShapeDtypeStruct((2, ROWS), F32),
        in_specs=[pl.BlockSpec(memory_space=pltpu.HBM)] * 3,
        out_specs=here,
        scratch_shapes=[
            vm((ROWS, D), F32),
            vm((ROWS,), jnp.int32),
            vm((1, ROWS), jnp.int32),
            vm((CH, COL, 32, HALF), BF16),
            vm((CH, COL, 32, HALF), BF16),
            vm((CH, PLANE, 16, HALF), BF16),
            vm((CH, PLANE, 16, HALF), BF16),
            vm((CH, PLANE, 16, HALF), BF16),
            vm((CH, COL, 32, HALF), BF16),
            vm((CH, COL, 32, HALF), BF16),
            vm((CH, PLANE, 16, D), BF16),
            vm((2, CH, PLANE, 16, D), BF16),
            vm((CH, PLANE, 16, D), BF16),
            vm((4, CH, 4, 16, D), BF16),
            vm((COL, 1, 128), F32),
            vm((COL, 1, 128), F32),
            vm((PLANE, 1, 128), F32),
            vm((PLANE, 1, 128), F32),
            vm((1, SLOTS), F32),
            vm((2, 1, SLOTS), F32),
            vm((1, SLOTS), F32),
            vm((CH, CR, 128), F32),
            vm((2, CH, CR, 128), F32),
            vm((2, 2, CH, CR, 128), F32),
            vm((2, 2, 8, SLOTS), F32),
            vm((PLANE, 4, 128), F32),
            vm((PLANE, 4, 128), F32),
            vm((COL, 1, 512), F32),
            vm((COL, 1, 512), F32),
            vm((CR, CR), BF16),
            vm((CR, CR), BF16),
            vm((128, SLOTS), BF16),
            vm((2 * SLOTS, 128), BF16),
            vm((128, 256), BF16),
            dma((4,)), dma((CH,)), dma((CH,)), dma((CH,)), dma((CH,)),
            dma((5,)), dma((5,)),
            dma((3, CH)), dma((3, CH)),
            dma((4, CH)), dma((4, CH)), dma((4, CH)),
            dma((2,)), dma((2,)),
            dma((4, CH)), dma((3,)),
        ],
        compiler_params=pltpu.CompilerParams(
            collective_id=0, has_side_effects=True, vmem_limit_bytes=VMEM_LIMIT
        ),
    )(embeddings, ranks, routes.reshape(1, ROWS))
    return out[0], out[1]


def solution(mesh):
    placed = (P(("group", "blk"), None), P(("group", "blk")), P(("group", "blk"), None))
    return jax.shard_map(
        body,
        mesh=mesh,
        in_specs=placed,
        out_specs=(P(("group", "blk")), P(("group", "blk"))),
        check_vma=False,
    )
```

```python
import jax
import jax.numpy as jnp
from jax import lax
from jax.experimental import pallas as pl
from jax.experimental.pallas import tpu as pltpu
from jax.sharding import PartitionSpec as P

MESH = pl.DeviceIdType.MESH
F32 = jnp.float32
BF16 = jnp.bfloat16

D = 1024
VMEM_LIMIT = 62 * 2**20
HALF = 512
ROWS = 384
SLOTS = 768
CH = 3
CR = 256
COL = 8
PLANE = 16

RINGS = (
    (0, 4, 8, 12, 13, 1, 5, 9, 10, 14, 2, 6, 7, 11, 15, 3),
    (0, 1, 2, 3, 7, 4, 5, 6, 10, 11, 8, 9, 13, 14, 15, 12),
)
PLACES = tuple(tuple(r.index(n) for n in range(PLANE)) for r in RINGS)
UPS = tuple(tuple(r[(r.index(n) + 1) % PLANE] for n in range(PLANE)) for r in RINGS)
DOWNS = tuple(tuple(r[(r.index(n) - 1) % PLANE] for n in range(PLANE)) for r in RINGS)
STRAIGHT = (11, 12, 11)
DETOURS = ((0, 1, 0), (0, -1, 1), (1, -1, 0), (1, 1, 1))


def span(share, q):
    first = STRAIGHT[q]
    middle = first + (PLANE - first + 1) // 2
    return (first, middle) if share == 0 else (middle, PLANE)


MIXED = (10, 1, 4, 3, 12, 2, 8, 5, 15, 7, 13, 6, 9, 14, 11)


def iota(shape, dim):
    return lax.broadcasted_iota(jnp.int32, shape, dim)


def hot(mask):
    return jnp.where(mask, 1.0, 0.0).astype(BF16)


def pick(x, onehot, parts):
    rows = x.shape[0]
    pieces = []
    for _ in range(parts):
        piece = x.astype(BF16)
        pieces.append(piece)
        x = x - piece.astype(F32)
    out = jnp.dot(jnp.concatenate(pieces, axis=0), onehot, preferred_element_type=F32)
    total = out[(parts - 1) * rows :]
    for p in range(parts - 2, -1, -1):
        total = total + out[p * rows : (p + 1) * rows]
    return total


def look(tables, odd, index):
    found = index * 0
    for i in range(PLANE):
        found = jnp.where(index == i, jnp.where(odd == 1, tables[1][i], tables[0][i]), found)
    return found


def rem(a, b):
    return lax.rem(a, b)


def device(n, z, core):
    x, y = lax.div(n, 4), rem(n, 4)
    return (rem(y, 2) * 2 + core, lax.div(y, 2) * 16 + x * 4 + z)


def each(first, last, act):
    for i in range(first, last):
        act(i)


def kernel(
    emb_hbm, ranks_hbm, routes_hbm, out,
    emb, ranks, routes, send1a, recv1a, send2a, send1b, recv1b, send2b, recv2b, own, left, right, relay,
    rk1s, rk1r, rk2s, rk2r, rk_own, rk_left, rk_right,
    lr_own, lr_left, acc_left, acc_right,
    b1s, b1r, b2s, b2r, by_chip, by_goal, m_home, m_back, unfold,
    ss_row, rs1a, rs2a, rs1b, rs2b, ss_rank, rs_rank,
    ss_ring, rs_ring, ss_leg1, rs_leg1, ss_leg2, ss_back, rs_back, loc, in_sem,
):
    loads = [
        pltpu.make_async_copy(src, dst, in_sem.at[i])
        for i, (src, dst) in enumerate(((routes_hbm, routes), (ranks_hbm, ranks), (emb_hbm, emb)))
    ]
    for load in loads:
        load.start()
    grp = lax.axis_index("group")
    blk = lax.axis_index("blk")
    z, core = rem(blk, 4), rem(grp, 2)
    n = rem(lax.div(blk, 4), 4) * 4 + lax.div(blk, 16) * 2 + lax.div(grp, 2)
    me = core * 4 + z
    odd = rem(z, 2)

    def col_dev(g):
        return device(n, rem(g, 4), lax.div(g, 4))

    def plane_dev(t):
        return device(t, z, core)

    sibling = device(n, z, 1 - core)

    barrier = pltpu.get_barrier_semaphore()

    def greet(to):
        pl.semaphore_signal(barrier, inc=1, device_id=to, device_id_type=MESH)

    for i in MIXED:
        greet(plane_dev(rem(n + i, PLANE)))
    each(1, COL, lambda i: greet(col_dev(rem(me + i, COL))))

    loads[0].wait()
    loads[1].wait()
    target = routes[...].reshape(1, ROWS)
    rank = ranks[...].reshape(1, ROWS).astype(F32) + 1.0
    spread = iota((128, ROWS), 0) == target
    before = hot(iota((ROWS, ROWS), 0) < iota((ROWS, ROWS), 1))
    count = jnp.dot(hot(spread), before, preferred_element_type=F32)
    slot = jnp.sum(jnp.where(spread, count, 0.0), axis=0, keepdims=True).astype(jnp.int32)
    cluster, block = target >> 5, target & 31
    goal = (block & 1) * 4 + cluster
    ring = block >> 1
    to_chip = look(RINGS, cluster & 1, ring)
    chunk, two = slot >> 1, slot & 1
    at_goal = iota((COL, ROWS), 0) == goal
    at_spot = hot(iota((128, ROWS), 0) == chunk * 32 + to_chip * 2 + two)
    at_back = hot(iota((128, ROWS), 0) == chunk * 32 + ring * 2 + two)
    ranks16 = jnp.concatenate([jnp.where(at_goal, rank, 0.0), jnp.zeros((COL, ROWS), F32)], axis=0)
    hi = ranks16.astype(BF16)
    lo = (ranks16 - hi.astype(F32)).astype(BF16)
    dims = (((1,), (1,)), ((), ()))
    packed = lax.dot_general(hi, at_spot, dims, preferred_element_type=F32) + lax.dot_general(
        lo, at_spot, dims, preferred_element_type=F32
    )
    for g in range(COL):
        rk1s[g] = packed[g : g + 1]
    loads[2].wait()
    e = emb[...]
    mean_square = jnp.mean(e * e, axis=-1, keepdims=True)
    unit = (e * lax.rsqrt(mean_square + 1e-06) * D ** (-0.5)).astype(BF16)

    def fill(q):
        for index, ref, first, shape in (
            (goal * 32 + to_chip * 2 + two, send1a, 0, (COL, 32, 256)),
            (to_chip * 16 + goal * 2 + two, send1b, HALF, (PLANE, 16, 256)),
        ):
            select = hot(iota((CR, ROWS), 0) == jnp.where(chunk == q, index, -1))
            for c in range(0, HALF, 256):
                rows = jnp.dot(select, unit[:, first + c : first + c + 256], preferred_element_type=F32)
                ref[q, :, :, c : c + 256] = rows.astype(BF16).reshape(shape)

    def copy(src, dst, send, recv, to):
        return pltpu.make_async_remote_copy(
            src_ref=src, dst_ref=dst, send_sem=send, recv_sem=recv, device_id=to, device_id_type=MESH
        )

    def rk1(i):
        g = rem(me + i, COL)
        return copy(rk1s.at[g], rk1r.at[me], ss_rank.at[0], rs_rank.at[0], col_dev(g))

    def rk2(i):
        t = rem(n + i, PLANE)
        return copy(rk2s.at[t], rk2r.at[n], ss_rank.at[1], rs_rank.at[1], plane_dev(t))

    def row1a(q, i):
        g = rem(me + i, COL)
        return copy(send1a.at[q, g], recv1a.at[q, me], ss_row.at[0], rs1a.at[q], col_dev(g))

    def row2a(q, i):
        t = rem(n + i, PLANE)
        return copy(send2a.at[q, t], own.at[q, n, :, pl.ds(0, HALF)], ss_row.at[1], rs2a.at[q], plane_dev(t))

    def row1b(q, i):
        t = rem(n + i, PLANE)
        return copy(send1b.at[q, t], recv1b.at[q, n], ss_row.at[2], rs1b.at[q], plane_dev(t))

    def row2b(q, i):
        g = rem(me + i, COL)
        return copy(send2b.at[q, g], recv2b.at[q, me], ss_row.at[3], rs2b.at[q], col_dev(g))

    def got_all(ref, sem):
        copy(ref, ref, ss_row.at[0], sem, sibling).wait_recv()

    def sent_all(ref, sem):
        copy(ref, ref, sem, rs_rank.at[0], sibling).wait_send()

    def stay1a(q):
        return pltpu.make_async_copy(send1a.at[q, me], recv1a.at[q, me], loc.at[0, q])

    def stay2a(q):
        return pltpu.make_async_copy(send2a.at[q, n], own.at[q, n, :, pl.ds(0, HALF)], loc.at[1, q])

    def stay1b(q):
        return pltpu.make_async_copy(send1b.at[q, n], recv1b.at[q, n], loc.at[2, q])

    def stay2b(q):
        return pltpu.make_async_copy(send2b.at[q, me], recv2b.at[q, me], loc.at[3, q])

    for q in range(CH):
        fill(q)

    s = look(PLACES, odd, n)
    up, down = look(UPS, odd, n), look(DOWNS, odd, n)
    beside = (look(UPS, 1 - odd, n), look(DOWNS, 1 - odd, n))

    a, b = iota((CR, CR), 0), iota((CR, CR), 1)
    by_chip[...] = hot(b == ((a & 15) >> 1) * 32 + (a >> 4) * 2 + (a & 1))
    by_goal[...] = hot(b == ((a & 31) >> 1) * 16 + (a >> 5) * 2 + (a & 1))
    lane = iota((128, SLOTS), 1)
    m_home[...] = hot(iota((128, SLOTS), 0) == (lane >> 8) * 16 + (lane & 15))
    lane = iota((CR, 128), 1)
    same = (lane & 15) == (iota((CR, 128), 0) & 15)
    for i in range(2 * CH):
        m_back[i * CR : (i + 1) * CR] = hot(same & (lane >> 4 == i))
    a, b = iota((128, 256), 0), iota((128, 256), 1)
    unfold[...] = hot(
        (a >> 4 == (b >> 7) * 3 + ((b & 127) >> 5)) & ((a & 1) == (b & 1)) & ((b & 127) < 96)
    )
    acc_left[...] = jnp.full(acc_left.shape, -1.0, F32)
    acc_right[...] = jnp.full(acc_right.shape, -1.0, F32)
    of_chip = ((iota((PLANE, SLOTS), 1) & 255) >> 4) == iota((PLANE, SLOTS), 0)

    pl.semaphore_wait(barrier, COL - 1 + PLANE - 1)
    each(1, COL, lambda i: rk1(i).start())
    for q in range(CH):
        for i, t in enumerate(MIXED):
            row1b(q, t).start()
            if i % 2 == 0 and i // 2 + 1 < COL:
                row1a(q, i // 2 + 1).start()
        stay1a(q).start()
        stay1b(q).start()

    rk1r[me] = rk1s[me]
    got_all(rk1r.at[pl.ds(0, COL - 1)], rs_rank.at[0])
    seen = jnp.concatenate([rk1r[g] for g in range(COL)], axis=0)
    lane = iota((PLANE, COL, 128), 2)
    wide = jnp.where(((lane & 31) >> 1) == iota((PLANE, COL, 128), 0), seen[None], 0.0)
    a, b = iota((128, 128), 0), iota((128, 128), 1)
    fold = hot((a >> 5 == b >> 4) & ((a & 1) == (b & 1)) & (a < 96))
    wide = pick(wide.reshape(128, 128), fold, 2).reshape(PLANE, COL, 128)
    wide = jnp.sum(jnp.where(((lane & 15) >> 1) == iota((PLANE, COL, 128), 1), wide, 0.0), axis=1)
    for t in range(PLANE):
        rk2s[t] = wide[t : t + 1]
    each(1, PLANE, lambda i: rk2(i).start())
    rk2r[n] = rk2s[n]

    def turn(order, src, dst, q, first, shape):
        for c in range(0, HALF, 256):
            rows = jnp.dot(order[...], src[q, :, :, c : c + 256].reshape(CR, 256), preferred_element_type=F32)
            dst[q, :, :, first + c : first + c + 256] = rows.astype(BF16).reshape(shape)

    def regroup(q):
        got_all(recv1b.at[q, pl.ds(0, PLANE - 1)], rs1b.at[q])
        stay1b(q).wait()
        turn(by_goal, recv1b, send2b, q, 0, (COL, 32, 256))
        each(1, COL, lambda i: row2b(q, i).start())
        stay2b(q).start()
        got_all(recv1a.at[q, pl.ds(0, COL - 1)], rs1a.at[q])
        stay1a(q).wait()
        turn(by_chip, recv1a, send2a, q, 0, (PLANE, 16, 256))
        for i in MIXED:
            row2a(q, i).start()
        stay2a(q).start()

    def straight(way, q):
        rows = pl.ds(0, STRAIGHT[q])
        return copy(
            own.at[q, rows], left.at[core, q, rows] if way == 0 else right.at[q, rows],
            ss_ring.at[way, q], rs_ring.at[way, q], plane_dev(up if way == 0 else down),
        )

    def leg1(d, q):
        _, side, share = DETOURS[d]
        first, last = span(share, q)
        return copy(
            own.at[q, pl.ds(first, last - first)], relay.at[d, q, pl.ds(0, last - first)],
            ss_leg1.at[d, q], rs_leg1.at[d, q], device(n, rem(z + 4 + side, 4), core),
        )

    def leg2(d, q):
        way, side, share = DETOURS[d]
        first, last = span(share, q)
        rows = pl.ds(first, last - first)
        return copy(
            relay.at[d, q, pl.ds(0, last - first)], left.at[core, q, rows] if way == 0 else right.at[q, rows],
            ss_leg2.at[d, q], rs_ring.at[way, q], device(beside[way], rem(z + 4 - side, 4), core),
        )

    def to_sibling(q, k):
        return copy(own.at[q] if k == 0 else left.at[1, q], left.at[k, q], ss_ring.at[2, q], rs_ring.at[2, q], sibling)

    def rk_ring(way):
        return copy(
            rk_own, rk_left.at[core] if way == 0 else rk_right,
            ss_rank.at[2 + way], rs_rank.at[2 + way], plane_dev(up if way == 0 else down),
        )

    def rk_sibling(k):
        return copy(rk_own if k == 0 else rk_left.at[1], rk_left.at[k], ss_rank.at[4], rs_rank.at[4], sibling)

    def spread_out(q):
        got_all(recv2b.at[q, pl.ds(0, COL - 1)], rs2b.at[q])
        stay2b(q).wait()
        turn(by_chip, recv2b, own, q, HALF, (PLANE, 16, 256))
        got_all(own.at[q, pl.ds(0, PLANE - 1), :, pl.ds(0, HALF)], rs2a.at[q])
        stay2a(q).wait()
        for d in range(len(DETOURS)):
            leg1(d, q).start()
        straight(0, q).start()
        straight(1, q).start()

        @pl.when(core == 0)
        def _():
            to_sibling(q, 0).start()

    def pass_on(q):
        for d in range(len(DETOURS)):
            leg1(d, q).wait_recv()
            leg2(d, q).start()

    regroup(0)

    got_all(rk2r.at[pl.ds(0, PLANE - 1)], rs_rank.at[1])
    got = jnp.concatenate([rk2r[t] for t in range(PLANE)], axis=0)
    got = pick(got, m_home[...], 2)
    got = jnp.sum(jnp.where(of_chip, got, 0.0), axis=0, keepdims=True)
    rk_own[...] = jnp.where(got > 0.0, got, jnp.nan)
    rk_ring(0).start()
    rk_ring(1).start()

    @pl.when(core == 0)
    def _():
        rk_sibling(0).start()

    regroup(1)
    spread_out(0)
    regroup(2)
    spread_out(1)
    pass_on(0)
    spread_out(2)
    pass_on(1)

    def stand(row):
        return jnp.broadcast_to(row, (128, SLOTS)).T.reshape(CH, CR, 128)

    lr_own[...] = stand(rk_own[...])

    def compare(rows, lr, other, rr, accs_left, accs_right):
        scores = lax.dot_general(
            jnp.concatenate(rows, axis=0), other, dims, preferred_element_type=F32
        )
        lefts = [[None, None] for _ in rows]
        for h in range(0, other.shape[0], 128):
            rank_right = rr[:, h : h + 128]
            rights = [None, None]
            for i, lr_i in enumerate(lr):
                part = scores[i * CR : (i + 1) * CR, h : h + 128]
                low = jnp.where(rank_right < lr_i, part, -1.0)
                high = jnp.where(rank_right > lr_i, part, -1.0)
                for el, new in enumerate((low, high)):
                    if accs_left is not None:
                        lefts[i][el] = new if lefts[i][el] is None else jnp.maximum(lefts[i][el], new)
                    new = jnp.max(new.reshape(32, 8, 128), axis=0)
                    rights[1 - el] = new if rights[1 - el] is None else jnp.maximum(rights[1 - el], new)
            for el in range(2):
                accs_right[el][:, h : h + 128] = jnp.maximum(accs_right[el][:, h : h + 128], rights[el])
        if accs_left is not None:
            for acc, new in zip(accs_left, lefts, strict=True):
                for el in range(2):
                    acc[el][...] = jnp.maximum(acc[el][...], new[el])

    compare(
        [own[q].reshape(CR, D) for q in range(CH)], [lr_own[q] for q in range(CH)], own[...].reshape(SLOTS, D), rk_own[...],
        None, [acc_right.at[0, el] for el in range(2)],
    )
    pass_on(2)

    rk_ring(0).wait_recv()

    @pl.when(core == 1)
    def _():
        rk_sibling(1).start()

    rk_ring(1).wait_recv()
    rk_sibling(0).wait_recv()
    for a in range(2):
        lr_left[a] = stand(rk_left[a])

    def compare_left(parts, side, first, last):
        other, rr = (own, rk_own) if side == 0 else (right, rk_right)
        cols = pl.ds(first * CR, (last - first) * CR)
        compare(
            [left[a, q].reshape(CR, D) for a, q in parts], [lr_left[a, q] for a, q in parts],
            other[first:last].reshape((last - first) * CR, D), rr[:, first * CR : last * CR],
            [[acc_left.at[a, el, q] for el in range(2)] for a, q in parts],
            [acc_right.at[side, el, :, cols] for el in range(2)],
        )

    for q in range(CH):
        got_all(left.at[core, q], rs_ring.at[0, q])

        @pl.when(core == 1)
        def _():
            to_sibling(q, 1).start()

        now = [(0, q), (1, q)]
        if q < CH - 1:
            got_all(left.at[1 - core, q], rs_ring.at[2, q])
            compare_left(now, 0, 0, CH)
        else:
            compare_left([(core, q)], 0, 0, CH)
            got_all(left.at[1 - core, q], rs_ring.at[2, q])
            compare_left([(1 - core, q)], 0, 0, CH)
        got_all(right.at[q], rs_ring.at[1, q])
        compare_left(now, 1, 0, q + 1)
        if q:
            compare_left([(a, p) for a in range(2) for p in range(q)], 1, q, q + 1)
        if q == 0:
            sent_all(send1a.at[:, pl.ds(0, COL - 1)], ss_row.at[0])
            sent_all(send2a.at[:, pl.ds(0, PLANE - 1)], ss_row.at[1])
            sent_all(send1b.at[:, pl.ds(0, PLANE - 1)], ss_row.at[2])
            sent_all(send2b.at[:, pl.ds(0, COL - 1)], ss_row.at[3])
            sent_all(rk1s.at[pl.ds(0, COL - 1)], ss_rank.at[0])
            sent_all(rk2s.at[pl.ds(0, PLANE - 1)], ss_rank.at[1])
            rk_ring(0).wait_send()
            rk_ring(1).wait_send()
            rk_sibling(0).wait_send()

    def back1(i):
        t = rem(n + i, PLANE)
        return copy(b1s.at[t], b1r.at[s], ss_back.at[0], rs_back.at[0], plane_dev(t))

    def back2(i):
        g = rem(me + i, COL)
        return copy(b2s.at[g], b2r.at[me], ss_back.at[1], rs_back.at[1], col_dev(g))

    def lie(acc):
        return jnp.max(acc.reshape(SLOTS, 128).T, axis=0, keepdims=True)

    def flat(acc):
        return jnp.max(acc, axis=0, keepdims=True)

    found = [[lie(acc_left[a, el]) for el in range(2)] for a in range(2)]
    found += [[flat(acc_right[r, el]) for el in range(2)] for r in range(2)]
    found = [jnp.concatenate([jnp.where(of_chip, m, 0.0) for m in f], axis=1) for f in found]
    found = pick(jnp.concatenate(found, axis=0), m_back[...], 3)
    for t in range(PLANE):
        for k in range(4):
            b1s[t, k : k + 1] = found[k * PLANE + t : k * PLANE + t + 1]
    each(1, PLANE, lambda i: back1(i).start())
    b1r[s] = b1s[n]
    got_all(b1r.at[pl.ds(0, PLANE - 1)], rs_back.at[0])

    def of(k):
        return jnp.concatenate([b1r[t, k : k + 1] for t in range(PLANE)], axis=0)

    def above(m):
        return jnp.concatenate([m[1:], m[:1]], axis=0)

    def below(m):
        return jnp.concatenate([m[PLANE - 1 :], m[: PLANE - 1]], axis=0)

    left0, left1, right0, right1 = of(0), above(of(1)), of(2), below(of(3))
    even = jnp.where(core == 0, jnp.maximum(jnp.maximum(right0, above(left0)), right1), left0)
    uneven = jnp.where(core == 0, left1, jnp.maximum(jnp.maximum(right0, left1), right1))
    wide = jnp.stack([even, uneven])[:, None]
    shape = (2, COL, PLANE, 128)
    wide = jnp.where(((iota(shape, 3) & 15) >> 1) == iota(shape, 1), wide, 0.0)
    wide = pick(wide.reshape(2 * COL * PLANE, 128), unfold[...], 3).reshape(2, COL, PLANE, 256)
    shape = (2, COL, PLANE, 256)
    wide = jnp.sum(jnp.where(((iota(shape, 3) & 31) >> 1) == iota(shape, 2), wide, 0.0), axis=2)
    wide = jnp.concatenate([wide[0], wide[1]], axis=1)
    for g in range(COL):
        b2s[g] = wide[g : g + 1]
    each(1, COL, lambda i: back2(i).start())
    b2r[me] = b2s[me]
    got_all(b2r.at[pl.ds(0, COL - 1)], rs_back.at[1])
    got = jnp.concatenate([b2r[g] for g in range(COL)], axis=0)
    got = jnp.maximum(got[:4], got[4:])
    got = jnp.concatenate([got[:, c : c + 128] for c in (0, 256, 128, 384)], axis=0)
    got = pick(got, at_back, 3)
    out[0:1] = jnp.sum(jnp.where(at_goal, got[:COL], 0.0), axis=0, keepdims=True)
    out[1:2] = jnp.sum(jnp.where(at_goal, got[COL:], 0.0), axis=0, keepdims=True)

    for q in range(CH):
        for way in range(2):
            sent_all(own.at[q, pl.ds(0, STRAIGHT[q])], ss_ring.at[way, q])
        sent_all(own.at[q], ss_ring.at[2, q])
        for d, (_, _, share) in enumerate(DETOURS):
            first, last = span(share, q)
            sent_all(own.at[q, pl.ds(first, last - first)], ss_leg1.at[d, q])
            sent_all(relay.at[d, q, pl.ds(0, last - first)], ss_leg2.at[d, q])
    sent_all(b1s.at[pl.ds(0, PLANE - 1)], ss_back.at[0])
    sent_all(b2s.at[pl.ds(0, COL - 1)], ss_back.at[1])


def body(embeddings, ranks, routes):
    dma = pltpu.SemaphoreType.DMA
    vm = pltpu.VMEM
    here = pl.BlockSpec(memory_space=vm)
    out = pl.pallas_call(
        kernel,
        out_shape=jax.ShapeDtypeStruct((2, ROWS), F32),
        in_specs=[pl.BlockSpec(memory_space=pltpu.HBM)] * 3,
        out_specs=here,
        scratch_shapes=[
            vm((ROWS, D), F32),
            vm((ROWS,), jnp.int32),
            vm((1, ROWS), jnp.int32),
            vm((CH, COL, 32, HALF), BF16),
            vm((CH, COL, 32, HALF), BF16),
            vm((CH, PLANE, 16, HALF), BF16),
            vm((CH, PLANE, 16, HALF), BF16),
            vm((CH, PLANE, 16, HALF), BF16),
            vm((CH, COL, 32, HALF), BF16),
            vm((CH, COL, 32, HALF), BF16),
            vm((CH, PLANE, 16, D), BF16),
            vm((2, CH, PLANE, 16, D), BF16),
            vm((CH, PLANE, 16, D), BF16),
            vm((4, CH, 4, 16, D), BF16),
            vm((COL, 1, 128), F32),
            vm((COL, 1, 128), F32),
            vm((PLANE, 1, 128), F32),
            vm((PLANE, 1, 128), F32),
            vm((1, SLOTS), F32),
            vm((2, 1, SLOTS), F32),
            vm((1, SLOTS), F32),
            vm((CH, CR, 128), F32),
            vm((2, CH, CR, 128), F32),
            vm((2, 2, CH, CR, 128), F32),
            vm((2, 2, 8, SLOTS), F32),
            vm((PLANE, 4, 128), F32),
            vm((PLANE, 4, 128), F32),
            vm((COL, 1, 512), F32),
            vm((COL, 1, 512), F32),
            vm((CR, CR), BF16),
            vm((CR, CR), BF16),
            vm((128, SLOTS), BF16),
            vm((2 * SLOTS, 128), BF16),
            vm((128, 256), BF16),
            dma((4,)), dma((CH,)), dma((CH,)), dma((CH,)), dma((CH,)),
            dma((5,)), dma((5,)),
            dma((3, CH)), dma((3, CH)),
            dma((4, CH)), dma((4, CH)), dma((4, CH)),
            dma((2,)), dma((2,)),
            dma((4, CH)), dma((3,)),
        ],
        compiler_params=pltpu.CompilerParams(
            collective_id=0, has_side_effects=True, vmem_limit_bytes=VMEM_LIMIT
        ),
    )(embeddings, ranks, routes.reshape(1, ROWS))
    return out[0], out[1]


def solution(mesh):
    placed = (P(("group", "blk"), None), P(("group", "blk")), P(("group", "blk"), None))
    return jax.shard_map(
        body,
        mesh=mesh,
        in_specs=placed,
        out_specs=(P(("group", "blk")), P(("group", "blk"))),
        check_vma=False,
    )
```
